256 devices in a mesh: row: 8 (over x, core), col: 32 (over y, z).
Axes of the slice: x: 4, y: 4, z: 8, core: 2. Of those that a mesh axis runs over, the one named last changes fastest.
Arguments:
- positions: float32 [3, 524288], P(None, ('row', 'col')), may hold values from 0 to 649
- velocities: float32 [3, 524288], P(None, ('row', 'col')), may hold values from -6 to 6
- chain_order: int32 [4096, 128], P(('row', 'col')), may hold values from 0 to 127, as said below
- tile_list: int32 [2, 20480], P(None, ('row', 'col')), may hold values from 0 to 511, as said below
Outputs:
- new_velocity: float32 [3, 524288], P(None, ('row', 'col'))
- new_position: float32 [3, 524288], P(None, ('row', 'col'))
The draws below stay inside these ranges and needn't reach their ends.
Inputs may be any that keep to these rules, and one draw needn't show every extreme that they name: `chain_order`: each row is a permutation of 0 to 127. `tile_list`: the first row names a block of the row group, below 512; the second a block of the column group, below 128; for k = 0 to 15, tile k of device (p, q) pairs that device's own block k with itself, its entries being q * 16 + k and p * 16 + k.
All inputs are finite; a program needn't handle non-finite values.
Results may differ from the reference program's by a relative error of at most 0.0003.
Values sent between devices are 32-bit elements; how exact they have to be, the bound alone decides.
A program may use at most 128 MiB of HBM per device.

```python
import jax
import jax.numpy as jnp
import numpy as np
from jax import lax

BLK = 128
CHAIN = 32
LINES_X = 4
LINES_Y = 4
BPD = 16
TILES = 80
GX = 128
GY = 32
BLOCKS = 4096
ATOMS = 524288
N_COL = 32
DEVICES = 256


def layout(key):
    key_y, key_x, key_chain = jax.random.split(key, 3)
    lines_y = jax.random.permutation(key_y, GY).astype(jnp.int32)
    lines_x = jax.random.permutation(key_x, GX).astype(jnp.int32)
    scores = jax.random.randint(key_chain, (BLOCKS, BLK), 0, 1 << 20, dtype=jnp.int32) * BLK
    scores = scores + jnp.arange(BLK, dtype=jnp.int32)[None, :]
    chain = jnp.argsort(scores, axis=1).astype(jnp.int32)
    return (lines_y, lines_x, chain)


def draw_positions(key, part):
    lines_y, lines_x, chain = layout(key)
    key = jax.random.fold_in(key, 11)
    slot = jnp.arange(BLOCKS, dtype=jnp.int32)
    device = slot // BPD
    local = slot % BPD
    grid_row = device // N_COL
    grid_column = device % N_COL
    block_y = lines_y[grid_row * LINES_Y + local // LINES_X]
    block_x = lines_x[grid_column * LINES_X + local % LINES_X]
    rank = jnp.argsort(chain, axis=1).astype(jnp.int32)
    layer = rank // 16
    within = rank % 16
    within = jnp.where(layer % 2 == 1, 15 - within, within)
    lane_y = within // 4
    lane_x = within % 4
    lane_x = jnp.where(lane_y % 2 == 1, 3 - lane_x, lane_x)
    sites = jnp.stack([block_x[:, None] * 4 + lane_x, block_y[:, None] * 4 + lane_y, layer]).astype(jnp.float32)
    jitter = jax.random.uniform(key, (3, BLOCKS, BLK), jnp.float32, -0.08, 0.08)
    return ((sites + 0.5) * 1.1 + jitter).reshape(3, BLOCKS * BLK)


def draw_chain_order(key, part):
    lines_y, lines_x, chain = layout(key)
    return chain


def draw_tile_list(key, part):
    lines_y, lines_x, chain = layout(key)
    inverse_y = jnp.zeros((GY,), jnp.int32).at[lines_y].set(jnp.arange(GY, dtype=jnp.int32))
    inverse_x = jnp.zeros((GX,), jnp.int32).at[lines_x].set(jnp.arange(GX, dtype=jnp.int32))
    anchor_x = jnp.repeat(jnp.arange(GX, dtype=jnp.int32), GY)
    anchor_y = jnp.tile(jnp.arange(GY, dtype=jnp.int32), GX)
    steps_x = jnp.asarray(np.array([0, 1, 0, 1, 1], dtype=np.int32))
    steps_y = jnp.asarray(np.array([0, 0, 1, 1, -1], dtype=np.int32))
    partner_x = (anchor_x[:, None] + steps_x[None, :]) % GX
    partner_y = (anchor_y[:, None] + steps_y[None, :] + GY) % GY
    anchor_x = jnp.broadcast_to(anchor_x[:, None], partner_x.shape)
    anchor_y = jnp.broadcast_to(anchor_y[:, None], partner_y.shape)

    def owner(place_x, place_y):
        line_y = inverse_y[place_y]
        line_x = inverse_x[place_x]
        return (line_y // LINES_Y, line_x // LINES_X, line_y % LINES_Y * LINES_X + line_x % LINES_X)
    anchor_row, anchor_column, anchor_local = owner(anchor_x, anchor_y)
    partner_row, partner_column, partner_local = owner(partner_x, partner_y)
    device = (anchor_row * N_COL + partner_column).reshape(-1)
    row_entry = (anchor_column * BPD + anchor_local).reshape(-1)
    column_entry = (partner_row * BPD + partner_local).reshape(-1)
    total = device.shape[0]
    self_tile = jnp.broadcast_to((jnp.arange(5, dtype=jnp.int32) == 0)[None, :], partner_x.shape).reshape(-1)
    local_key = anchor_local.reshape(-1)
    rank_key = jnp.where(self_tile, local_key, total + jnp.arange(total, dtype=jnp.int32))
    order = jnp.argsort(device * (2 * total) + rank_key).astype(jnp.int32)
    return jnp.stack([row_entry[order], column_entry[order]]).astype(jnp.int32)


def level_of(key, dims, pieces, low, largest):
    gain, own = 1.0, jax.random.fold_in(key, 6)
    for axis_at, parts in pieces:
        heights = jnp.exp(jax.random.uniform(jax.random.fold_in(own, axis_at), (parts,), jnp.float32, low / len(pieces), largest / len(pieces)))
        gain = gain * jnp.repeat(heights, dims[axis_at] // parts).reshape([-1 if axis == axis_at else 1 for axis in range(len(dims))])
    return gain


def bell_draw(own_key, extent, scale, most, cuts=(), kind=jnp.bfloat16):
    entries = scale * jax.random.normal(own_key, extent, jnp.float32)
    if cuts:
        entries = entries * level_of(own_key, extent, cuts, -0.22, 0.18)
    return jnp.clip(entries, -most, most).astype(kind)


def setup_inputs(seed: int = 0) -> dict:
    key_of = jax.random.split(jax.random.key(seed), 5)
    return {
        "positions": draw_positions(jax.random.fold_in(key_of[4], 71), 0),
        "velocities": bell_draw(key_of[1], (3, ATOMS), 1.0, 6.0, ((1, 256),), jnp.float32),
        "chain_order": draw_chain_order(jax.random.fold_in(key_of[4], 71), 0),
        "tile_list": draw_tile_list(jax.random.fold_in(key_of[4], 71), 0),
    }


cutoff = 2.5
spacing = 1.1
spring = 30.0
bond_reach = 1.5
time_step = 0.005
shift_force = 24.0 * (2.0 * cutoff ** (-13) - cutoff ** (-7))

def pair_terms(row_atoms, column_atoms, same_block, periods):
    offset = row_atoms[:, :, None] - column_atoms[:, None, :]
    offset = offset - periods * jnp.floor(offset / periods + 0.5)
    squared = lax.optimization_barrier(jnp.sum(offset * offset, axis=0))
    atom_count = row_atoms.shape[1]
    diagonal = jnp.eye(atom_count, dtype=bool) & same_block
    inside = (squared < cutoff * cutoff) & jnp.logical_not(diagonal)
    guarded = jnp.where(diagonal, 1.0, squared)
    inverse = 1.0 / guarded
    cubed = inverse * inverse * inverse
    magnitude = 24.0 * inverse * cubed * (2.0 * cubed - 1.0) - shift_force * jnp.sqrt(inverse)
    magnitude = jnp.where(inside, magnitude, 0.0)
    pair_force = offset * magnitude[None]
    keep_column = jnp.where(same_block, 0.0, 1.0)
    return (lax.optimization_barrier(jnp.sum(pair_force, axis=2)), -lax.optimization_barrier(jnp.sum(pair_force, axis=1)) * keep_column)

def fene(block_positions, chain):
    block_count = block_positions.shape[1]
    ordered = jnp.take_along_axis(block_positions, chain[None], axis=2)
    bond_vector = ordered[:, :, 1:] - ordered[:, :, :-1]
    squared = lax.optimization_barrier(jnp.sum(bond_vector * bond_vector, axis=0))
    rank_next = jnp.arange(1, BLK, dtype=jnp.int32)
    bonded = rank_next % CHAIN != 0
    coefficient = -spring / jnp.maximum(1.0 - squared / (bond_reach * bond_reach), 0.3)
    coefficient = jnp.where(bonded[None, :], coefficient, 0.0)
    pulled = bond_vector * coefficient[None]
    chain_force = jnp.pad(pulled, ((0, 0), (0, 0), (1, 0))) - jnp.pad(pulled, ((0, 0), (0, 0), (0, 1)))
    block_rows = jnp.arange(block_count, dtype=jnp.int32)[:, None]
    return jnp.zeros_like(block_positions).at[:, block_rows, chain].set(chain_force)

def reference(positions, velocities, chain_order, tile_list):
    blocks = positions.reshape(3, -1, BLK)
    periods = jnp.asarray([4.0 * spacing * GX, 4.0 * spacing * GY, 8.0 * spacing]).astype(positions.dtype).reshape(3, 1, 1)
    tile_table = tile_list.reshape(2, DEVICES, TILES)

    def one_device(forces, device):
        grid_row = device // N_COL
        grid_column = device % N_COL
        row_pick = grid_row * (N_COL * BPD) + tile_table[0, device]
        column_entry = tile_table[1, device]
        column_pick = (column_entry // BPD * N_COL + grid_column) * BPD + column_entry % BPD
        same_block = row_pick == column_pick
        row_part, column_part = jax.vmap(pair_terms, in_axes=(1, 1, 0, None), out_axes=1)(blocks[:, row_pick], blocks[:, column_pick], same_block, periods)
        forces = forces.at[:, row_pick].add(row_part)
        forces = forces.at[:, column_pick].add(column_part)
        return (forces, None)
    forces, _ = lax.scan(one_device, jnp.zeros_like(blocks), jnp.arange(DEVICES, dtype=jnp.int32))
    forces = forces + fene(blocks, chain_order)
    new_velocity = velocities + time_step * forces.reshape(3, -1)
    new_position = positions + time_step * new_velocity
    return (new_velocity, new_position)
```

```python
import functools

import jax
import jax.numpy as jnp
from jax import lax
from jax.experimental import pallas as pl
from jax.experimental.pallas import tpu as pltpu
from jax.sharding import PartitionSpec as P

BLK = 128
CHAIN = 32
LINES_X = 4
LINES_Y = 4
OWN = 16
FAR = 64
GROUP = 8
BATCHES = FAR // GROUP
MESH = pl.DeviceIdType.MESH

cutoff = 2.5
spacing = 1.1
spring = 30.0
bond_reach = 1.5
time_step = 0.005
shift_force = 24.0 * (2.0 * cutoff ** (-13) - cutoff ** (-7))


def to_phase(x, period):
    per_unit = 2.0**32 / period
    whole = round(per_unit)
    n = jnp.floor(x)
    rest = n * jnp.float32(per_unit - whole) + (x - n) * jnp.float32(per_unit)
    return n.astype(jnp.int32) * jnp.int32(whole) + rest.astype(jnp.int32)


def pair(row, column, scales, extra=None):
    d = [(a - b).astype(jnp.float32) * s for a, b, s in zip(row, column, scales)]
    squared = d[0] * d[0] + d[1] * d[1] + d[2] * d[2]
    if extra is not None:
        squared = squared + extra
    t = lax.rsqrt(squared)
    s = t * t
    cubed = s * s * s
    magnitude = (s * cubed) * (cubed - 0.5) - jnp.float32(shift_force / 48.0) * t
    magnitude = jnp.where(squared < cutoff * cutoff, magnitude, 0.0)
    return [v * magnitude for v in d]


def skew(row, first):
    wide = jnp.broadcast_to(row, (8, BLK))
    return pltpu.roll(wide, first, 1, stride=1, stride_axis=0)


def unskew(total, first, index):
    if first:
        total = pltpu.roll(total, BLK - first, 1)
    back = jnp.take_along_axis(total, index, axis=1, mode="promise_in_bounds")
    return jnp.sum(back, axis=0, keepdims=True)


def tile(row, column, first, count, scales, extra, last_mask, index):
    row = [jnp.broadcast_to(v, (8, BLK)) for v in row]
    base = [skew(v, first) for v in column]
    to_row = to_column = None
    for r in range(count):
        now = base if r == 0 else [pltpu.roll(v, 8 * r, 1) for v in base]
        f = pair(row, now, scales, extra if r == 0 else None)
        to_row = f if to_row is None else [a + b for a, b in zip(to_row, f)]
        if last_mask is not None and r == count - 1:
            f = [jnp.where(last_mask, v, 0.0) for v in f]
        g = f if r == 0 else [pltpu.roll(v, BLK - 8 * r, 1) for v in f]
        to_column = g if to_column is None else [a + b for a, b in zip(to_column, g)]
    return (
        [jnp.sum(v, axis=0, keepdims=True) for v in to_row],
        [unskew(v, first, index) for v in to_column],
    )


def spread(one_hot, parts):
    return lax.dot_general(
        one_hot,
        parts,
        (((1,), (0,)), ((), ())),
        precision=lax.Precision.HIGHEST,
        preferred_element_type=jnp.float32,
    )


def kernel(
    NR, NY, NZ,
    tl, pos, chain, tlv, out,
    gath, colg, own_u, row_x, col_x, row_u, col_u, own_f, inv, meta, prs, cparts,
    totals, coltot, rs2, crs,
    ag_send, ag_recv, fw_send, rg_send, rg_recv, mt_send, mt_recv,
    r1_send, r1_recv, r2_send, r2_recv, rc_send, rc_recv,
):
    periods = [
        4.0 * spacing * LINES_X * NY * NZ,
        4.0 * spacing * LINES_Y * NR,
        8.0 * spacing,
    ]
    scales = [jnp.float32(v / 2.0**32) for v in periods]
    p = lax.axis_index("row")
    q = lax.axis_index("col")
    y = q // NZ
    z = q % NZ

    def at_z(d):
        return (p, y * NZ + lax.rem(z + d, NZ))

    def at_y(d):
        return (p, lax.rem(y + d, NY) * NZ + z)

    def at_row(d):
        return (lax.rem(p + d, NR), q)

    barrier = pltpu.get_barrier_semaphore()
    peers = (
        [at_z(d) for d in range(1, NZ)]
        + [at_y(d) for d in range(1, NY)]
        + [at_row(d) for d in range(1, NR)]
    )
    for peer in peers:
        pl.semaphore_signal(barrier, inc=1, device_id=peer, device_id_type=MESH)

    for d in range(3):
        for b in range(OWN):
            v = pos[d : d + 1, b * BLK : (b + 1) * BLK]
            gath[q, d, b : b + 1, :] = v
            colg[p, d, b : b + 1, :] = v
    meta[y] = jnp.full((8, BLK), -1.0, jnp.float32)
    meta[y, 0:1, 0:FAR] = tlv[0:1, OWN : OWN + FAR].astype(jnp.float32)
    pl.semaphore_wait(barrier, len(peers))

    def copy(src, dst, send, recv, peer):
        return pltpu.make_async_remote_copy(
            src_ref=src, dst_ref=dst, send_sem=send, recv_sem=recv,
            device_id=peer, device_id_type=MESH,
        )

    def z_step(i):
        half = i // 2 + 1
        return lax.rem(half + (i % 2) * (NZ - 2 * half), NZ)

    def ag_copy(d):
        return copy(gath.at[q], gath.at[q], ag_send.at[d - 1], ag_recv.at[q], at_z(d))

    def chunk_arrived(slot):
        copy(gath.at[slot], gath.at[slot], ag_send.at[0], ag_recv.at[slot], at_z(1)).wait_recv()

    def forward(slot, j, d):
        return copy(gath.at[slot], gath.at[slot], fw_send.at[j, d - 1], ag_recv.at[slot], at_y(d))

    def row_copy(d):
        return copy(colg.at[p], colg.at[p], rg_send.at[d - 1], rg_recv.at[p], at_row(d))

    def meta_copy(d):
        return copy(meta.at[y], meta.at[y], mt_send.at[d - 1], mt_recv.at[y], at_y(d))

    y_order = [1, NY - 1] + list(range(2, NY - 1)) if NY > 2 else [1]
    z_order = []
    for i in range(1, NZ):
        d = (i + 1) // 2 if i % 2 else NZ - i // 2
        z_order.append(d)
    for d in z_order[:2]:
        ag_copy(d).start()
    for d in y_order:
        forward(q, 0, d).start()
    for d in z_order[2:]:
        ag_copy(d).start()
    for d in range(1, NR):
        row_copy(d).start()
    for d in y_order:
        meta_copy(d).start()

    lane = lax.broadcasted_iota(jnp.int32, (8, BLK), 1)
    sub = lax.broadcasted_iota(jnp.int32, (8, BLK), 0)
    index = (lane + sub) & (BLK - 1)

    order = chain[...]
    x = [gath[q, d] for d in range(3)]
    for d in range(3):
        own_u[d] = to_phase(x[d], periods[d])
    order_t = jnp.transpose(order.astype(jnp.float32))
    lane_f = lax.broadcasted_iota(jnp.int32, (BLK, BLK), 1).astype(jnp.float32)
    sub_f = lax.broadcasted_iota(jnp.int32, (BLK, BLK), 0).astype(jnp.float32)
    for b in range(OWN):
        hit = order_t[:, b : b + 1] == lane_f
        inv[b : b + 1, :] = jnp.sum(jnp.where(hit, sub_f, 0.0), axis=0, keepdims=True)
    back = inv[...].astype(jnp.int32)
    ordered = [jnp.take_along_axis(v, order, axis=1, mode="promise_in_bounds") for v in x]
    bond = [pltpu.roll(v, BLK - 1, 1) - v for v in ordered]
    squared = bond[0] * bond[0] + bond[1] * bond[1] + bond[2] * bond[2]
    rank = lax.broadcasted_iota(jnp.int32, (OWN, BLK), 1) + 1
    strength = -spring / jnp.maximum(1.0 - squared / (bond_reach * bond_reach), 0.3)
    strength = jnp.where(rank % CHAIN != 0, strength, 0.0)
    for d in range(3):
        pulled = bond[d] * strength
        along = pltpu.roll(pulled, 1, 1) - pulled
        own_f[d] = jnp.take_along_axis(along, back, axis=1, mode="promise_in_bounds")

    def self_tile(k):
        u = [own_u[d, pl.ds(k, 1), :] for d in range(3)]
        to_row, to_column = tile(u, u, 1, BLK // 16, scales, None, sub < 7, index)
        for d in range(3):
            own_f[d, pl.ds(k, 1), :] += 48.0 * (to_row[d] - to_column[d])

    def self_step(i, carry):
        self_tile(2 * i)
        self_tile(2 * i + 1)
        slot = y * NZ + lax.rem(z + z_step(i), NZ)
        chunk_arrived(slot)
        for d in y_order:
            forward(slot, i + 1, d).start()
        return carry

    lax.fori_loop(0, NZ - 1, self_step, 0)

    def self_rest(i, carry):
        self_tile(2 * i)
        self_tile(2 * i + 1)
        return carry

    lax.fori_loop(NZ - 1, OWN // 2, self_rest, 0)

    def y_arrived(i, carry):
        for d in y_order:
            chunk_arrived(lax.rem(y + d, NY) * NZ + lax.rem(z + i, NZ))
        return carry

    lax.fori_loop(0, NZ, y_arrived, 0)
    for d in range(1, NR):
        slot = lax.rem(p + d, NR)
        copy(colg.at[slot], colg.at[slot], rg_send.at[0], rg_recv.at[slot], at_row(1)).wait_recv()

    def stage(i, carry):
        for j in range(GROUP):
            t = i * GROUP + j
            r = tl[0, OWN + t]
            c = tl[1, OWN + t]
            for d in range(3):
                row_x[d, pl.ds(t, 1), :] = gath[r >> 4, d, pl.ds(r & 15, 1), :]
                col_x[d, pl.ds(t, 1), :] = colg[c >> 4, d, pl.ds(c & 15, 1), :]
        return carry

    lax.fori_loop(0, BATCHES, stage, 0)

    def phase(i, carry):
        at = pl.ds(pl.multiple_of(i * GROUP, GROUP), GROUP)
        for d in range(3):
            row_u[d, at, :] = to_phase(row_x[d, at, :], periods[d])
            col_u[d, at, :] = to_phase(col_x[d, at, :], periods[d])
        return carry

    lax.fori_loop(0, BATCHES, phase, 0)

    def far_tile(b, j):
        t = b * GROUP + j
        r = tl[0, OWN + t]
        c = tl[1, OWN + t]
        same = p * (NY * NZ * OWN) + r == ((c >> 4) * (NY * NZ) + q) * OWN + (c & 15)
        extra = jnp.where((sub == 0) & same, 1e6, 0.0)
        u = [row_u[d, pl.ds(t, 1), :] for d in range(3)]
        v = [col_u[d, pl.ds(t, 1), :] for d in range(3)]
        to_row, to_column = tile(u, v, 0, BLK // 8, scales, extra, None, index)
        for d in range(3):
            prs[y, b, d, pl.ds(j, 1), :] = to_row[d]
            cparts[b, d, pl.ds(j, 1), :] = to_column[d]

    def r1_copy(b, d):
        return copy(
            prs.at[y, b], prs.at[y, b], r1_send.at[b, d - 1], r1_recv.at[y, b], at_y(d)
        )

    def batch(b, carry):
        def two(j, inner):
            far_tile(b, 2 * j)
            far_tile(b, 2 * j + 1)
            return inner

        lax.fori_loop(0, GROUP // 2, two, 0)
        for d in y_order:
            r1_copy(b, d).start()
        return carry

    lax.fori_loop(0, BATCHES, batch, 0)

    r = tlv[0:1, OWN : OWN + FAR]
    c = tlv[1:2, OWN : OWN + FAR]
    same = p * (NY * NZ * OWN) + r == ((c >> 4) * (NY * NZ) + q) * OWN + (c & 15)
    rows = lax.broadcasted_iota(jnp.int32, (NR * OWN, FAR), 0)
    minus = jnp.where((rows == c) & jnp.logical_not(same), -1.0, 0.0)
    for d in range(3):
        full = spread(minus, cparts[:, d].reshape(FAR, BLK))
        coltot[:, d] = full.reshape(NR, OWN, BLK)

    def rc_copy(d):
        to = lax.rem(p + d, NR)
        return copy(coltot.at[to], crs.at[p], rc_send.at[d - 1], rc_recv.at[p], at_row(d))

    for d in range(1, NR):
        rc_copy(d).start()

    for d in y_order:
        slot = lax.rem(y + d, NY)
        copy(meta.at[slot], meta.at[slot], mt_send.at[0], mt_recv.at[slot], at_y(1)).wait_recv()

    def r1_arrived(b, carry):
        for d in y_order:
            slot = lax.rem(y + d, NY)
            copy(
                prs.at[slot, b], prs.at[slot, b], r1_send.at[0, 0], r1_recv.at[slot, b], at_y(1)
            ).wait_recv()
        return carry

    lax.fori_loop(0, BATCHES, r1_arrived, 0)
    names = jnp.concatenate([meta[i, 0:1, 0:FAR] for i in range(NY)], axis=1)
    mine = lax.broadcasted_iota(jnp.int32, (NZ * OWN, NY * FAR), 0) + y * (NZ * OWN)
    plus = jnp.where(mine.astype(jnp.float32) == names, 1.0, 0.0)
    for d in range(3):
        full = spread(plus, prs[:, :, d].reshape(NY * FAR, BLK))
        totals[:, d] = full.reshape(NZ, OWN, BLK)

    def r2_copy(d):
        to = lax.rem(z + d, NZ)
        return copy(totals.at[to], rs2.at[z], r2_send.at[d - 1], r2_recv.at[z], at_z(d))

    for d in reversed(z_order):
        r2_copy(d).start()

    acc = [coltot[p, d] for d in range(3)]
    for i in range(1, NR):
        slot = lax.rem(p + i, NR)
        copy(coltot.at[slot], crs.at[slot], rc_send.at[0], rc_recv.at[slot], at_row(1)).wait_recv()
        acc = [acc[d] + crs[slot, d] for d in range(3)]
    acc = [acc[d] + totals[z, d] for d in range(3)]
    for i in z_order:
        slot = lax.rem(z + i, NZ)
        copy(totals.at[slot], rs2.at[slot], r2_send.at[0], r2_recv.at[slot], at_z(1)).wait_recv()
        acc = [acc[d] + rs2[slot, d] for d in range(3)]
    for d in range(3):
        total = 48.0 * acc[d] + own_f[d]
        for b in range(OWN):
            out[d : d + 1, b * BLK : (b + 1) * BLK] = total[b : b + 1, :]

    for d in range(1, NZ):
        ag_copy(d).wait_send()
        r2_copy(d).wait_send()
    for d in range(1, NR):
        row_copy(d).wait_send()
        rc_copy(d).wait_send()
    for d in range(1, NY):
        meta_copy(d).wait_send()

    def left(i, carry):
        for d in range(1, NY):
            forward(q, i, d).wait_send()
        return carry

    lax.fori_loop(0, NZ, left, 0)

    def left_parts(b, carry):
        for d in range(1, NY):
            r1_copy(b, d).wait_send()
        return carry

    lax.fori_loop(0, BATCHES, left_parts, 0)


def on_device(NR, NY, NZ, positions, velocities, chain_order, tile_list):
    f32 = jnp.float32
    dma = pltpu.SemaphoreType.DMA
    vmem = pl.BlockSpec(memory_space=pltpu.VMEM)
    forces = pl.pallas_call(
        functools.partial(kernel, NR, NY, NZ),
        out_shape=jax.ShapeDtypeStruct(positions.shape, f32),
        in_specs=[pl.BlockSpec(memory_space=pltpu.SMEM), vmem, vmem, vmem],
        out_specs=vmem,
        scratch_shapes=[
            pltpu.VMEM((NY * NZ, 3, OWN, BLK), f32),
            pltpu.VMEM((NR, 3, OWN, BLK), f32),
            pltpu.VMEM((3, OWN, BLK), jnp.int32),
            pltpu.VMEM((3, FAR, BLK), f32),
            pltpu.VMEM((3, FAR, BLK), f32),
            pltpu.VMEM((3, FAR, BLK), jnp.int32),
            pltpu.VMEM((3, FAR, BLK), jnp.int32),
            pltpu.VMEM((3, OWN, BLK), f32),
            pltpu.VMEM((OWN, BLK), f32),
            pltpu.VMEM((NY, 8, BLK), f32),
            pltpu.VMEM((NY, BATCHES, 3, GROUP, BLK), f32),
            pltpu.VMEM((BATCHES, 3, GROUP, BLK), f32),
            pltpu.VMEM((NZ, 3, OWN, BLK), f32),
            pltpu.VMEM((NR, 3, OWN, BLK), f32),
            pltpu.VMEM((NZ, 3, OWN, BLK), f32),
            pltpu.VMEM((NR, 3, OWN, BLK), f32),
            dma((NZ - 1,)),
            dma((NY * NZ,)),
            dma((NZ, NY - 1)),
            dma((NR - 1,)),
            dma((NR,)),
            dma((NY - 1,)),
            dma((NY,)),
            dma((BATCHES, NY - 1)),
            dma((NY, BATCHES)),
            dma((NZ - 1,)),
            dma((NZ,)),
            dma((NR - 1,)),
            dma((NR,)),
        ],
        compiler_params=pltpu.CompilerParams(
            collective_id=0, has_side_effects=True, vmem_limit_bytes=32 * 1024 * 1024
        ),
    )(tile_list, positions, chain_order, tile_list)
    new_velocity = velocities + time_step * forces
    new_position = positions + time_step * new_velocity
    return (new_velocity, new_position)


def solution(mesh, NZ=8):
    in_specs = (
        P(None, ("row", "col")),
        P(None, ("row", "col")),
        P(("row", "col"), None),
        P(None, ("row", "col")),
    )
    out_specs = (P(None, ("row", "col")), P(None, ("row", "col")))
    return jax.shard_map(
        functools.partial(on_device, mesh.shape["row"], mesh.shape["col"] // NZ, NZ),
        mesh=mesh,
        in_specs=in_specs,
        out_specs=out_specs,
        check_vma=False,
    )
```

```python
import functools

import jax
import jax.numpy as jnp
from jax import lax
from jax.experimental import pallas as pl
from jax.experimental.pallas import tpu as pltpu
from jax.sharding import PartitionSpec as P

BLK = 128
CHAIN = 32
LINES_X = 4
LINES_Y = 4
OWN = 16
FAR = 64
GROUP = 8
BATCHES = FAR // GROUP
MESH = pl.DeviceIdType.MESH

cutoff = 2.5
spacing = 1.1
spring = 30.0
bond_reach = 1.5
time_step = 0.005
shift_force = 24.0 * (2.0 * cutoff ** (-13) - cutoff ** (-7))
strength = -shift_force
unit = (48.0 / strength) ** (1.0 / 13.0)
middle = 0.5 * unit**6


def to_phase(x, period):
    per_unit = 2.0**32 / period
    whole = round(per_unit)
    n = jnp.floor(x)
    rest = n * jnp.float32(per_unit - whole) + (x - n) * jnp.float32(per_unit)
    return n.astype(jnp.int32) * jnp.int32(whole) + rest.astype(jnp.int32)


def pair(row, column, scales, extra=None):
    d = [(a - b).astype(jnp.float32) * s for a, b, s in zip(row, column, scales)]
    squared = d[0] * d[0] + d[1] * d[1] + d[2] * d[2]
    if extra is not None:
        squared = squared + extra
    t = lax.rsqrt(squared)
    s = t * t
    cubed = s * s * s
    magnitude = (s * cubed) * (cubed - jnp.float32(middle)) + t
    magnitude = jnp.where(squared < jnp.float32((cutoff / unit) ** 2), magnitude, 0.0)
    return [v * magnitude for v in d]


def skew(row, first):
    wide = jnp.broadcast_to(row, (8, BLK))
    return pltpu.roll(wide, first, 1, stride=1, stride_axis=0)


def meet(rows, columns, scales, extra, last_mask):
    to_rows = [None] * len(rows)
    to_columns = [None] * len(columns)
    for i, row in enumerate(rows):
        for j, column in enumerate(columns):
            f = pair(row, column, scales, extra if i + j == 0 else None)
            to_rows[i] = f if j == 0 else [x + v for x, v in zip(to_rows[i], f)]
            if last_mask is not None and (i, j) == (len(rows) - 1, len(columns) - 1):
                f = [jnp.where(last_mask, v, 0.0) for v in f]
            to_columns[j] = f if i == 0 else [x + v for x, v in zip(to_columns[j], f)]
    return to_rows, to_columns


def settle_row(parts):
    total = parts[0]
    for i, v in enumerate(parts[1:], 1):
        total = total + pltpu.roll(v, 8 * i, 1)
    return total


def settle_column(parts, shifts):
    total = None
    for v, shift in zip(parts, shifts):
        v = pltpu.roll(v, BLK - shift, 1) if shift else v
        total = v if total is None else total + v
    return total


def unskew(total, index):
    return jnp.take_along_axis(total, index, axis=1, mode="promise_in_bounds")


def fold(total):
    return jnp.sum(total, axis=0, keepdims=True)


FAR_SHIFTS = (0, 32, 64, 96)
SELF_SHIFTS = (1, 17, 33, 49)


def spread(one_hot, parts):
    return lax.dot_general(
        one_hot,
        parts,
        (((1,), (0,)), ((), ())),
        precision=lax.Precision.HIGHEST,
        preferred_element_type=jnp.float32,
    )


def kernel(
    NR, NY, NZ,
    tl, pos, chain, tlv, out,
    gath, colg, own_u, row_x, col_x, row_u, col_u, skewed, held, rolled, own_f, inv, meta, prs, cparts,
    totals, coltot, rs2, crs,
    ag_send, ag_recv, fw_send, rg_send, rg_recv, mt_send, mt_recv,
    r1_send, r1_recv, r2_send, r2_recv, rc_send, rc_recv,
):
    periods = [
        4.0 * spacing * LINES_X * NY * NZ,
        4.0 * spacing * LINES_Y * NR,
        8.0 * spacing,
    ]
    scales = [jnp.float32(v / 2.0**32 / unit) for v in periods]
    p = lax.axis_index("row")
    q = lax.axis_index("col")
    y = q // NZ
    z = q % NZ

    def at_z(d):
        return (p, y * NZ + lax.rem(z + d, NZ))

    def at_y(d):
        return (p, lax.rem(y + d, NY) * NZ + z)

    def at_row(d):
        return (lax.rem(p + d, NR), q)

    barrier = pltpu.get_barrier_semaphore()
    peers = (
        [at_z(d) for d in range(1, NZ)]
        + [at_y(d) for d in range(1, NY)]
        + [at_row(d) for d in range(1, NR)]
    )
    for peer in peers:
        pl.semaphore_signal(barrier, inc=1, device_id=peer, device_id_type=MESH)

    for d in range(3):
        for b in range(OWN):
            v = pos[d : d + 1, b * BLK : (b + 1) * BLK]
            gath[q, d, b : b + 1, :] = v
            colg[p, d, b : b + 1, :] = v
    meta[y] = jnp.full((8, BLK), -1.0, jnp.float32)
    meta[y, 0:1, 0:FAR] = tlv[0:1, OWN : OWN + FAR].astype(jnp.float32)
    pl.semaphore_wait(barrier, len(peers))

    def copy(src, dst, send, recv, peer):
        return pltpu.make_async_remote_copy(
            src_ref=src, dst_ref=dst, send_sem=send, recv_sem=recv,
            device_id=peer, device_id_type=MESH,
        )

    def z_step(i):
        half = i // 2 + 1
        return lax.rem(half + (i % 2) * (NZ - 2 * half), NZ)

    def ag_copy(d):
        return copy(gath.at[q], gath.at[q], ag_send.at[d - 1], ag_recv.at[q], at_z(d))

    def chunk_arrived(slot):
        copy(gath.at[slot], gath.at[slot], ag_send.at[0], ag_recv.at[slot], at_z(1)).wait_recv()

    def forward(slot, j, d):
        return copy(gath.at[slot], gath.at[slot], fw_send.at[j, d - 1], ag_recv.at[slot], at_y(d))

    def row_copy(d):
        return copy(colg.at[p], colg.at[p], rg_send.at[d - 1], rg_recv.at[p], at_row(d))

    def meta_copy(d):
        return copy(meta.at[y], meta.at[y], mt_send.at[d - 1], mt_recv.at[y], at_y(d))

    y_order = [1, NY - 1] + list(range(2, NY - 1)) if NY > 2 else [1]
    z_order = []
    for i in range(1, NZ):
        d = (i + 1) // 2 if i % 2 else NZ - i // 2
        z_order.append(d)
    for d in z_order[:2]:
        ag_copy(d).start()
    for d in y_order:
        forward(q, 0, d).start()
    for d in z_order[2:]:
        ag_copy(d).start()
    for d in range(1, NR):
        row_copy(d).start()
    for d in y_order:
        meta_copy(d).start()

    lane = lax.broadcasted_iota(jnp.int32, (8, BLK), 1)
    sub = lax.broadcasted_iota(jnp.int32, (8, BLK), 0)
    index = (lane + sub) & (BLK - 1)

    order = chain[...]
    x = [gath[q, d] for d in range(3)]
    for d in range(3):
        own_u[d] = to_phase(x[d], periods[d])
    order_t = jnp.transpose(order.astype(jnp.float32))
    lane_f = lax.broadcasted_iota(jnp.int32, (BLK, BLK), 1).astype(jnp.float32)
    sub_f = lax.broadcasted_iota(jnp.int32, (BLK, BLK), 0).astype(jnp.float32)
    for b in range(OWN):
        hit = order_t[:, b : b + 1] == lane_f
        inv[b : b + 1, :] = jnp.sum(jnp.where(hit, sub_f, 0.0), axis=0, keepdims=True)
    back = inv[...].astype(jnp.int32)
    ordered = [jnp.take_along_axis(v, order, axis=1, mode="promise_in_bounds") for v in x]
    bond = [pltpu.roll(v, BLK - 1, 1) - v for v in ordered]
    squared = bond[0] * bond[0] + bond[1] * bond[1] + bond[2] * bond[2]
    rank = lax.broadcasted_iota(jnp.int32, (OWN, BLK), 1) + 1
    stiffness = -spring / jnp.maximum(1.0 - squared / (bond_reach * bond_reach), 0.3)
    stiffness = jnp.where(rank % CHAIN != 0, stiffness, 0.0)
    for d in range(3):
        pulled = bond[d] * stiffness
        along = pltpu.roll(pulled, 1, 1) - pulled
        own_f[d] = jnp.take_along_axis(along, back, axis=1, mode="promise_in_bounds")

    def self_tile(k):
        u = [own_u[d, pl.ds(k, 1), :] for d in range(3)]
        wide = [jnp.broadcast_to(v, (8, BLK)) for v in u]
        rows = [wide, [pltpu.roll(v, BLK - 8, 1) for v in wide]]
        columns = [[skew(v, shift) for v in u] for shift in SELF_SHIFTS]
        to_rows, to_columns = meet(rows, columns, scales, None, sub < 7)
        for d in range(3):
            force = settle_row([v[d] for v in to_rows])
            force -= unskew(settle_column([v[d] for v in to_columns], SELF_SHIFTS), index)
            own_f[d, pl.ds(k, 1), :] += strength * fold(force)

    def self_step(i, carry):
        self_tile(2 * i)
        self_tile(2 * i + 1)
        slot = y * NZ + lax.rem(z + z_step(i), NZ)
        chunk_arrived(slot)
        for d in y_order:
            forward(slot, i + 1, d).start()
        return carry

    lax.fori_loop(0, NZ - 1, self_step, 0)

    def self_rest(i, carry):
        self_tile(2 * i)
        self_tile(2 * i + 1)
        return carry

    lax.fori_loop(NZ - 1, OWN // 2, self_rest, 0)

    def y_arrived(i, carry):
        for d in y_order:
            chunk_arrived(lax.rem(y + d, NY) * NZ + lax.rem(z + i, NZ))
        return carry

    lax.fori_loop(0, NZ, y_arrived, 0)
    for d in range(1, NR):
        slot = lax.rem(p + d, NR)
        copy(colg.at[slot], colg.at[slot], rg_send.at[0], rg_recv.at[slot], at_row(1)).wait_recv()

    def stage(i, carry):
        for j in range(GROUP):
            t = i * GROUP + j
            r = tl[0, OWN + t]
            c = tl[1, OWN + t]
            for d in range(3):
                row_x[d, pl.ds(t, 1), :] = gath[r >> 4, d, pl.ds(r & 15, 1), :]
                col_x[d, pl.ds(t, 1), :] = colg[c >> 4, d, pl.ds(c & 15, 1), :]
        return carry

    lax.fori_loop(0, BATCHES, stage, 0)

    def phase(i, carry):
        at = pl.ds(pl.multiple_of(i * GROUP, GROUP), GROUP)
        for d in range(3):
            u = to_phase(row_x[d, at, :], periods[d])
            row_u[0, d, at, :] = u
            for k in range(1, 4):
                row_u[k, d, at, :] = pltpu.roll(u, BLK - 8 * k, 1)
            col_u[d, at, :] = to_phase(col_x[d, at, :], periods[d])
        return carry

    lax.fori_loop(0, BATCHES, phase, 0)

    def head(t):
        for d in range(3):
            u = col_u[d, pl.ds(t, 1), :]
            for k, shift in enumerate(FAR_SHIFTS):
                skewed[k, d] = skew(u, shift)

    def r1_copy(b, d):
        return copy(
            prs.at[y, b], prs.at[y, b], r1_send.at[b, d - 1], r1_recv.at[y, b], at_y(d)
        )

    def far_step(t, carry):
        before = jnp.maximum(t - 2, 0)
        for d in range(3):
            at = pl.ds(before % GROUP, 1)
            prs[y, before // GROUP, d, at, :] = fold(rolled[d])
            cparts[before // GROUP, d, at, :] = fold(unskew(rolled[3 + d], index))
        for d in range(3):
            rolled[d] = settle_row([held[k, d] for k in range(4)])
            rolled[3 + d] = settle_column([held[4 + k, d] for k in range(4)], FAR_SHIFTS)
        now = jnp.minimum(t, FAR - 1)
        r = tl[0, OWN + now]
        c = tl[1, OWN + now]
        same = p * (NY * NZ * OWN) + r == ((c >> 4) * (NY * NZ) + q) * OWN + (c & 15)
        extra = jnp.where((sub == 0) & same, 1e6, 0.0)
        rows = [
            [jnp.broadcast_to(row_u[k, d, pl.ds(now, 1), :], (8, BLK)) for d in range(3)]
            for k in range(4)
        ]
        columns = [[skewed[k, d] for d in range(3)] for k in range(4)]
        to_rows, to_columns = meet(rows, columns, scales, extra, None)
        head(jnp.minimum(t + 1, FAR - 1))
        for k in range(4):
            for d in range(3):
                held[k, d] = to_rows[k][d]
                held[4 + k, d] = to_columns[k][d]
        return carry

    def batch(b, carry):
        start = b * GROUP
        lax.fori_loop(start, start + jnp.where(b < BATCHES, GROUP, 2), far_step, 0)

        @pl.when(b > 0)
        def _():
            for d in y_order:
                r1_copy(b - 1, d).start()

        return carry

    held[...] = jnp.zeros_like(held)
    rolled[...] = jnp.zeros_like(rolled)
    head(0)
    lax.fori_loop(0, BATCHES + 1, batch, 0)

    r = tlv[0:1, OWN : OWN + FAR]
    c = tlv[1:2, OWN : OWN + FAR]
    same = p * (NY * NZ * OWN) + r == ((c >> 4) * (NY * NZ) + q) * OWN + (c & 15)
    rows = lax.broadcasted_iota(jnp.int32, (NR * OWN, FAR), 0)
    minus = jnp.where((rows == c) & jnp.logical_not(same), -1.0, 0.0)
    for d in range(3):
        full = spread(minus, cparts[:, d].reshape(FAR, BLK))
        coltot[:, d] = full.reshape(NR, OWN, BLK)

    def rc_copy(d):
        to = lax.rem(p + d, NR)
        return copy(coltot.at[to], crs.at[p], rc_send.at[d - 1], rc_recv.at[p], at_row(d))

    for d in range(1, NR):
        rc_copy(d).start()

    for d in y_order:
        slot = lax.rem(y + d, NY)
        copy(meta.at[slot], meta.at[slot], mt_send.at[0], mt_recv.at[slot], at_y(1)).wait_recv()

    def r1_arrived(b, carry):
        for d in y_order:
            slot = lax.rem(y + d, NY)
            copy(
                prs.at[slot, b], prs.at[slot, b], r1_send.at[0, 0], r1_recv.at[slot, b], at_y(1)
            ).wait_recv()
        return carry

    lax.fori_loop(0, BATCHES, r1_arrived, 0)
    names = jnp.concatenate([meta[i, 0:1, 0:FAR] for i in range(NY)], axis=1)
    mine = lax.broadcasted_iota(jnp.int32, (NZ * OWN, NY * FAR), 0) + y * (NZ * OWN)
    plus = jnp.where(mine.astype(jnp.float32) == names, 1.0, 0.0)
    for d in range(3):
        full = spread(plus, prs[:, :, d].reshape(NY * FAR, BLK))
        totals[:, d] = full.reshape(NZ, OWN, BLK)

    def r2_copy(d):
        to = lax.rem(z + d, NZ)
        return copy(totals.at[to], rs2.at[z], r2_send.at[d - 1], r2_recv.at[z], at_z(d))

    for d in reversed(z_order):
        r2_copy(d).start()

    acc = [coltot[p, d] for d in range(3)]
    for i in range(1, NR):
        slot = lax.rem(p + i, NR)
        copy(coltot.at[slot], crs.at[slot], rc_send.at[0], rc_recv.at[slot], at_row(1)).wait_recv()
        acc = [acc[d] + crs[slot, d] for d in range(3)]
    acc = [acc[d] + totals[z, d] for d in range(3)]
    for i in z_order:
        slot = lax.rem(z + i, NZ)
        copy(totals.at[slot], rs2.at[slot], r2_send.at[0], r2_recv.at[slot], at_z(1)).wait_recv()
        acc = [acc[d] + rs2[slot, d] for d in range(3)]
    for d in range(3):
        total = strength * acc[d] + own_f[d]
        for b in range(OWN):
            out[d : d + 1, b * BLK : (b + 1) * BLK] = total[b : b + 1, :]

    for d in range(1, NZ):
        ag_copy(d).wait_send()
        r2_copy(d).wait_send()
    for d in range(1, NR):
        row_copy(d).wait_send()
        rc_copy(d).wait_send()
    for d in range(1, NY):
        meta_copy(d).wait_send()

    def left(i, carry):
        for d in range(1, NY):
            forward(q, i, d).wait_send()
        return carry

    lax.fori_loop(0, NZ, left, 0)

    def left_parts(b, carry):
        for d in range(1, NY):
            r1_copy(b, d).wait_send()
        return carry

    lax.fori_loop(0, BATCHES, left_parts, 0)


def on_device(NR, NY, NZ, positions, velocities, chain_order, tile_list):
    f32 = jnp.float32
    dma = pltpu.SemaphoreType.DMA
    vmem = pl.BlockSpec(memory_space=pltpu.VMEM)
    forces = pl.pallas_call(
        functools.partial(kernel, NR, NY, NZ),
        out_shape=jax.ShapeDtypeStruct(positions.shape, f32),
        in_specs=[pl.BlockSpec(memory_space=pltpu.SMEM), vmem, vmem, vmem],
        out_specs=vmem,
        scratch_shapes=[
            pltpu.VMEM((NY * NZ, 3, OWN, BLK), f32),
            pltpu.VMEM((NR, 3, OWN, BLK), f32),
            pltpu.VMEM((3, OWN, BLK), jnp.int32),
            pltpu.VMEM((3, FAR, BLK), f32),
            pltpu.VMEM((3, FAR, BLK), f32),
            pltpu.VMEM((4, 3, FAR, BLK), jnp.int32),
            pltpu.VMEM((3, FAR, BLK), jnp.int32),
            pltpu.VMEM((4, 3, 8, BLK), jnp.int32),
            pltpu.VMEM((8, 3, 8, BLK), f32),
            pltpu.VMEM((6, 8, BLK), f32),
            pltpu.VMEM((3, OWN, BLK), f32),
            pltpu.VMEM((OWN, BLK), f32),
            pltpu.VMEM((NY, 8, BLK), f32),
            pltpu.VMEM((NY, BATCHES, 3, GROUP, BLK), f32),
            pltpu.VMEM((BATCHES, 3, GROUP, BLK), f32),
            pltpu.VMEM((NZ, 3, OWN, BLK), f32),
            pltpu.VMEM((NR, 3, OWN, BLK), f32),
            pltpu.VMEM((NZ, 3, OWN, BLK), f32),
            pltpu.VMEM((NR, 3, OWN, BLK), f32),
            dma((NZ - 1,)),
            dma((NY * NZ,)),
            dma((NZ, NY - 1)),
            dma((NR - 1,)),
            dma((NR,)),
            dma((NY - 1,)),
            dma((NY,)),
            dma((BATCHES, NY - 1)),
            dma((NY, BATCHES)),
            dma((NZ - 1,)),
            dma((NZ,)),
            dma((NR - 1,)),
            dma((NR,)),
        ],
        compiler_params=pltpu.CompilerParams(
            collective_id=0, has_side_effects=True, vmem_limit_bytes=32 * 1024 * 1024
        ),
    )(tile_list, positions, chain_order, tile_list)
    new_velocity = velocities + time_step * forces
    new_position = positions + time_step * new_velocity
    return (new_velocity, new_position)


def solution(mesh, NZ=8):
    in_specs = (
        P(None, ("row", "col")),
        P(None, ("row", "col")),
        P(("row", "col"), None),
        P(None, ("row", "col")),
    )
    out_specs = (P(None, ("row", "col")), P(None, ("row", "col")))
    return jax.shard_map(
        functools.partial(on_device, mesh.shape["row"], mesh.shape["col"] // NZ, NZ),
        mesh=mesh,
        in_specs=in_specs,
        out_specs=out_specs,
        check_vma=False,
    )
```

```python
import functools

import jax
import jax.numpy as jnp
from jax import lax
from jax.experimental import pallas as pl
from jax.experimental.pallas import tpu as pltpu
from jax.sharding import PartitionSpec as P

BLK = 128
CHAIN = 32
LINES_X = 4
LINES_Y = 4
OWN = 16
FAR = 64
GROUP = 8
BATCHES = FAR // GROUP
MESH = pl.DeviceIdType.MESH

cutoff = 2.5
spacing = 1.1
spring = 30.0
bond_reach = 1.5
time_step = 0.005
shift_force = 24.0 * (2.0 * cutoff ** (-13) - cutoff ** (-7))
strength = -shift_force
unit = (48.0 / strength) ** (1.0 / 13.0)
middle = 0.5 * unit**6


def to_phase(x, period):
    per_unit = 2.0**32 / period
    whole = round(per_unit)
    n = jnp.floor(x)
    rest = n * jnp.float32(per_unit - whole) + (x - n) * jnp.float32(per_unit)
    return n.astype(jnp.int32) * jnp.int32(whole) + rest.astype(jnp.int32)


def pair(row, column, scales, extra=None):
    d = [(a - b).astype(jnp.float32) * s for a, b, s in zip(row, column, scales)]
    squared = d[0] * d[0] + d[1] * d[1] + d[2] * d[2]
    if extra is not None:
        squared = squared + extra
    t = lax.rsqrt(squared)
    s = t * t
    cubed = s * s * s
    magnitude = (s * cubed) * (cubed - jnp.float32(middle)) + t
    magnitude = jnp.where(squared < jnp.float32((cutoff / unit) ** 2), magnitude, 0.0)
    return [v * magnitude for v in d]


def skew(row, first):
    wide = jnp.broadcast_to(row, (8, BLK))
    return pltpu.roll(wide, first, 1, stride=1, stride_axis=0)


def meet(rows, columns, scales, extra, last_mask):
    to_rows = [None] * len(rows)
    to_columns = [None] * len(columns)
    for i, row in enumerate(rows):
        for j, column in enumerate(columns):
            f = pair(row, column, scales, extra if i + j == 0 else None)
            to_rows[i] = f if j == 0 else [x + v for x, v in zip(to_rows[i], f)]
            if last_mask is not None and (i, j) == (len(rows) - 1, len(columns) - 1):
                f = [jnp.where(last_mask, v, 0.0) for v in f]
            to_columns[j] = f if i == 0 else [x + v for x, v in zip(to_columns[j], f)]
    return to_rows, to_columns


def settle_row(parts):
    total = parts[0]
    for i, v in enumerate(parts[1:], 1):
        total = total + pltpu.roll(v, 8 * i, 1)
    return total


def settle_column(parts, shifts):
    total = None
    for v, shift in zip(parts, shifts):
        v = pltpu.roll(v, BLK - shift, 1) if shift else v
        total = v if total is None else total + v
    return total


def unskew(total, index):
    return jnp.take_along_axis(total, index, axis=1, mode="promise_in_bounds")


def fold(total):
    return jnp.sum(total, axis=0, keepdims=True)


FAR_SHIFTS = (0, 32, 64, 96)
SELF_SHIFTS = (1, 17, 33, 49)


def spread(one_hot, parts):
    total = None
    for _ in range(3):
        piece = parts.astype(jnp.bfloat16)
        parts = parts - piece.astype(jnp.float32)
        product = jnp.dot(one_hot, piece, preferred_element_type=jnp.float32)
        total = product if total is None else total + product
    return total


def kernel(
    NR, NY, NZ,
    tl_any, pos_any, chain_any, out,
    tl, tlv, pos, chain, gath, colg, gath_u, colg_u, rowed, skewed, held, rolled,
    own_f, inv, meta, prs, cparts, totals, coltot, rs2, crs,
    in_sem, sent, a_recv, b_recv, group_recv, r1_recv,
):
    periods = [
        4.0 * spacing * LINES_X * NY * NZ,
        4.0 * spacing * LINES_Y * NR,
        8.0 * spacing,
    ]
    scales = [jnp.float32(v / 2.0**32 / unit) for v in periods]
    p = lax.axis_index("row")
    q = lax.axis_index("col")
    y = q >> (NZ.bit_length() - 1)
    z = q & (NZ - 1)

    def at_z(d):
        return (p, y * NZ + ((z + d) & (NZ - 1)))

    def at_y(d):
        return (p, ((y + d) & (NY - 1)) * NZ + z)

    def at_row(d):
        return ((p + d) & (NR - 1), q)

    barrier = pltpu.get_barrier_semaphore()
    peers = (
        [at_z(d) for d in sorted(range(1, NZ), key=lambda d: -min(d, NZ - d))]
        + [at_y(d) for d in range(1, NY)]
        + [at_row(d) for d in range(1, NR)]
    )
    for peer in peers:
        pl.semaphore_signal(barrier, inc=1, device_id=peer, device_id_type=MESH)
    reads = [
        pltpu.make_async_copy(src, dst, in_sem.at[i])
        for i, (src, dst) in enumerate(
            [(pos_any, pos), (chain_any, chain), (tl_any, tl), (tl_any, tlv)]
        )
    ]
    for read in reads:
        read.start()

    y_order = [1, NY - 1] + list(range(2, NY - 1)) if NY > 2 else [1]
    z_order = [(i + 1) // 2 if i % 2 else NZ - i // 2 for i in range(1, NZ)]

    def copy(src, dst, send, recv, peer):
        return pltpu.make_async_remote_copy(
            src_ref=src, dst_ref=dst, send_sem=send, recv_sem=recv,
            device_id=peer, device_id_type=MESH,
        )

    def arrived(sem, like):
        pltpu.make_async_copy(like, like, sem).wait()

    def slot_of(u, v):
        return ((y + u) & (NY - 1)) * NZ + ((z + v) & (NZ - 1))

    def a_part(slot, send, recv, peer):
        ref = gath.at[slot, pl.ds(0, 2)]
        return copy(ref, ref, send, recv, peer)

    def b_part(slot, send, recv, peer):
        ref = gath.at[slot, 2]
        return copy(ref, ref, send, recv, peer)

    def a_first(d):
        return a_part(q, sent.at[0], a_recv.at[0, z], at_z(d))

    def a_then(k, d):
        far_z = (z + k) & (NZ - 1)
        return a_part(y * NZ + far_z, sent.at[1], a_recv.at[1, far_z], at_y(d))

    def b_first(d):
        return b_part(q, sent.at[2], b_recv.at[0, y], at_y(d))

    def b_then(k, d):
        return b_part(((y + k) & (NY - 1)) * NZ + z, sent.at[3], b_recv.at[1, z], at_z(d))

    def row_copy(d):
        return copy(colg.at[p], colg.at[p], sent.at[4], group_recv.at[0], at_row(d))

    def meta_copy(d):
        return copy(meta.at[y], meta.at[y], sent.at[5], group_recv.at[1], at_y(d))

    def a_phase(slot):
        for d in range(2):
            gath_u[slot, d] = to_phase(gath[slot, d], periods[d])

    def b_phase(slot):
        gath_u[slot, 2] = to_phase(gath[slot, 2], periods[2])

    reads[0].wait()
    for b in range(OWN):
        for d in range(3):
            v = pos[d : d + 1, b * BLK : (b + 1) * BLK]
            gath[q, d, b : b + 1, :] = v
            colg[p, d, b : b + 1, :] = v
    lane = lax.broadcasted_iota(jnp.int32, (8, BLK), 1)
    sub = lax.broadcasted_iota(jnp.int32, (8, BLK), 0)
    index = (lane + sub) & (BLK - 1)

    pl.semaphore_wait(barrier, len(peers))
    for d in y_order:
        b_first(d).start()
    for d in z_order[:2]:
        a_first(d).start()
    for d in y_order:
        a_then(0, d).start()
    for d in z_order[2:]:
        a_first(d).start()
    for d in z_order:
        b_then(0, d).start()
    for d in range(1, NR):
        row_copy(d).start()
    for read in reads[1:]:
        read.wait()
    meta[y] = jnp.full((8, BLK), -1.0, jnp.float32)
    meta[y, 0:1, 0:FAR] = tlv[0:1, OWN : OWN + FAR].astype(jnp.float32)

    for d in y_order:
        meta_copy(d).start()

    for d in range(3):
        u = to_phase(gath[q, d], periods[d])
        gath_u[q, d] = u
        colg_u[p, d] = u

    def pass_a(i, carry):
        k = z_step(i)
        slot = slot_of(0, k)
        arrived(a_recv.at[0, (z + k) & (NZ - 1)], gath.at[slot, pl.ds(0, 2)])
        for d in y_order:
            a_then(k, d).start()
        a_phase(slot)
        return carry

    def pass_b(k):
        slot = slot_of(k, 0)
        arrived(b_recv.at[0, (y + k) & (NY - 1)], gath.at[slot, 2])
        for d in z_order:
            b_then(k, d).start()
        b_phase(slot)

    def z_step(i):
        half = (i >> 1) + 1
        return (half + (i & 1) * (NZ - 2 * half)) & (NZ - 1)

    lax.fori_loop(0, min(2, NZ - 1), pass_a, 0)
    for k in y_order[:2]:
        pass_b(k)
    lax.fori_loop(min(2, NZ - 1), min(4, NZ - 1), pass_a, 0)
    for k in y_order[2:]:
        pass_b(k)
    lax.fori_loop(min(4, NZ - 1), NZ - 1, pass_a, 0)

    arrived(group_recv.at[0], colg.at[pl.ds(0, NR - 1)])
    for i in range(1, NR):
        slot = (p + i) & (NR - 1)
        for d in range(3):
            colg_u[slot, d] = to_phase(colg[slot, d], periods[d])

    def a_rest(k):
        arrived(a_recv.at[1, (z + k) & (NZ - 1)], gath.at[pl.ds(0, NY - 1), pl.ds(0, 2)])
        for d in y_order:
            a_phase(slot_of(d, k))

    def rest(i, carry):
        k = z_step(i)
        arrived(b_recv.at[1, (z + k) & (NZ - 1)], gath.at[pl.ds(0, NY), 2])
        for d in range(NY):
            b_phase(slot_of(d, k))
        a_rest(k)
        return carry

    a_rest(0)
    lax.fori_loop(0, NZ - 1, rest, 0)

    def head(t, rowed, skewed):
        r = tl[0, OWN + t]
        c = tl[1, OWN + t]
        for d in range(3):
            row = jnp.broadcast_to(gath_u[r >> 4, d, pl.ds(r & 15, 1), :], (8, BLK))
            rowed[0, d] = row
            for k in range(1, 4):
                rowed[k, d] = pltpu.roll(row, BLK - 8 * k, 1)
            column = colg_u[c >> 4, d, pl.ds(c & 15, 1), :]
            for k, shift in enumerate(FAR_SHIFTS):
                skewed[k, d] = skew(column, shift)

    def r1_copy(b, d):
        return copy(
            prs.at[b, y], prs.at[b, y], sent.at[6], r1_recv.at[b // (BATCHES - 1)], at_y(d)
        )

    def far_step(t, rowed, skewed, next_rowed, next_skewed):
        before = jnp.maximum(t - 2, 0)
        for d in range(3):
            at = pl.ds(before % GROUP, 1)
            prs[before // GROUP, y, d, at, :] = fold(rolled[d])
            cparts[before // GROUP, d, at, :] = fold(unskew(rolled[3 + d], index))
        for d in range(3):
            rolled[d] = settle_row([held[k, d] for k in range(4)])
            rolled[3 + d] = settle_column([held[4 + k, d] for k in range(4)], FAR_SHIFTS)
        now = jnp.minimum(t, FAR - 1)
        r = tl[0, OWN + now]
        c = tl[1, OWN + now]
        same = p * (NY * NZ * OWN) + r == ((c >> 4) * (NY * NZ) + q) * OWN + (c & 15)
        extra = jnp.where((sub == 0) & same, 1e6, 0.0)
        rows = [[rowed[k, d] for d in range(3)] for k in range(4)]
        columns = [[skewed[k, d] for d in range(3)] for k in range(4)]
        to_rows, to_columns = meet(rows, columns, scales, extra, None)
        head(jnp.minimum(t + 1, FAR - 1), next_rowed, next_skewed)
        for k in range(4):
            for d in range(3):
                held[k, d] = to_rows[k][d]
                held[4 + k, d] = to_columns[k][d]

    def far_steps(i, carry):
        far_step(2 * i, rowed.at[0], skewed.at[0], rowed.at[1], skewed.at[1])
        far_step(2 * i + 1, rowed.at[1], skewed.at[1], rowed.at[0], skewed.at[0])
        return carry

    def batch(b, carry):
        start = b * (GROUP // 2)
        lax.fori_loop(start, start + jnp.where(b < BATCHES, GROUP // 2, 1), far_steps, 0)

        @pl.when(b > 0)
        def _():
            for d in y_order:
                r1_copy(b - 1, d).start()

        return carry

    held[...] = jnp.zeros_like(held)
    rolled[...] = jnp.zeros_like(rolled)
    head(0, rowed.at[0], skewed.at[0])
    lax.fori_loop(0, BATCHES + 1, batch, 0)

    r = tlv[0:1, OWN : OWN + FAR]
    c = tlv[1:2, OWN : OWN + FAR]
    same = p * (NY * NZ * OWN) + r == ((c >> 4) * (NY * NZ) + q) * OWN + (c & 15)
    rows = lax.broadcasted_iota(jnp.int32, (NR * OWN, FAR), 0)
    minus = jnp.where((rows == c) & jnp.logical_not(same), -1.0, 0.0).astype(jnp.bfloat16)
    for d in range(3):
        full = spread(minus, cparts[:, d].reshape(FAR, BLK))
        coltot[:, d] = full.reshape(NR, OWN, BLK)

    def rc_copy(d):
        to = (p + d) & (NR - 1)
        return copy(coltot.at[to], crs.at[p], sent.at[7], group_recv.at[2], at_row(d))

    for d in range(1, NR):
        rc_copy(d).start()

    arrived(sent.at[0], gath.at[pl.ds(0, NZ - 1), pl.ds(0, 2)])
    arrived(sent.at[1], gath.at[pl.ds(0, NZ * (NY - 1)), pl.ds(0, 2)])
    arrived(sent.at[2], gath.at[pl.ds(0, NY - 1), 2])
    arrived(sent.at[3], gath.at[pl.ds(0, NY * (NZ - 1)), 2])
    arrived(sent.at[4], colg.at[pl.ds(0, NR - 1)])
    arrived(sent.at[5], meta.at[pl.ds(0, NY - 1)])

    def self_tile(k):
        u = [gath_u[q, d, pl.ds(k, 1), :] for d in range(3)]
        wide = [jnp.broadcast_to(v, (8, BLK)) for v in u]
        rows = [wide, [pltpu.roll(v, BLK - 8, 1) for v in wide]]
        columns = [[skew(v, shift) for v in u] for shift in SELF_SHIFTS]
        to_rows, to_columns = meet(rows, columns, scales, None, sub < 7)
        for d in range(3):
            force = settle_row([v[d] for v in to_rows])
            force -= unskew(settle_column([v[d] for v in to_columns], SELF_SHIFTS), index)
            own_f[d, pl.ds(k, 1), :] = strength * fold(force)

    def self_tiles(i, carry):
        self_tile(2 * i)
        self_tile(2 * i + 1)
        return carry

    lax.fori_loop(0, OWN // 2, self_tiles, 0)

    arrived(group_recv.at[1], meta.at[pl.ds(0, NY - 1)])

    def chosen(lo, hi):
        names = jnp.concatenate(
            [meta[i, 0:1, b * GROUP : (b + 1) * GROUP] for b in range(lo, hi) for i in range(NY)],
            axis=1,
        )
        count = NY * GROUP * (hi - lo)
        mine = lax.broadcasted_iota(jnp.int32, (NZ * OWN, count), 0) + y * (NZ * OWN)
        return jnp.where(mine.astype(jnp.float32) == names, 1.0, 0.0).astype(jnp.bfloat16)

    last = BATCHES - 1
    early = chosen(0, last)
    late = chosen(last, BATCHES)
    arrived(r1_recv.at[0], prs.at[pl.ds(0, last), pl.ds(0, NY - 1)])
    for d in range(3):
        full = spread(early, prs[0:last, :, d].reshape(last * NY * GROUP, BLK))
        totals[:, d] = full.reshape(NZ, OWN, BLK)
    arrived(r1_recv.at[1], prs.at[last, pl.ds(0, NY - 1)])
    for d in range(3):
        full = spread(late, prs[last, :, d].reshape(NY * GROUP, BLK))
        totals[:, d] += full.reshape(NZ, OWN, BLK)

    def r2_copy(d):
        to = (z + d) & (NZ - 1)
        return copy(totals.at[to], rs2.at[z], sent.at[8], group_recv.at[3], at_z(d))

    for d in reversed(z_order):
        r2_copy(d).start()

    x = [gath[q, d] for d in range(3)]
    order = chain[...]
    order_t = jnp.transpose(order.astype(jnp.float32))
    lane_f = lax.broadcasted_iota(jnp.int32, (BLK, BLK), 1).astype(jnp.float32)
    sub_f = lax.broadcasted_iota(jnp.int32, (BLK, BLK), 0).astype(jnp.float32)
    for b in range(OWN):
        hit = order_t[:, b : b + 1] == lane_f
        inv[b : b + 1, :] = jnp.sum(jnp.where(hit, sub_f, 0.0), axis=0, keepdims=True)
    back = inv[...].astype(jnp.int32)
    ordered = [jnp.take_along_axis(v, order, axis=1, mode="promise_in_bounds") for v in x]
    bond = [pltpu.roll(v, BLK - 1, 1) - v for v in ordered]
    squared = bond[0] * bond[0] + bond[1] * bond[1] + bond[2] * bond[2]
    rank = lax.broadcasted_iota(jnp.int32, (OWN, BLK), 1) + 1
    stiffness = -spring / jnp.maximum(1.0 - squared / (bond_reach * bond_reach), 0.3)
    stiffness = jnp.where(rank % CHAIN != 0, stiffness, 0.0)
    for d in range(3):
        pulled = bond[d] * stiffness
        along = pltpu.roll(pulled, 1, 1) - pulled
        own_f[d] += jnp.take_along_axis(along, back, axis=1, mode="promise_in_bounds")

    arrived(sent.at[6], prs.at[:, pl.ds(0, NY - 1)])
    arrived(sent.at[7], crs.at[pl.ds(0, NR - 1)])
    arrived(group_recv.at[2], crs.at[pl.ds(0, NR - 1)])
    acc = [coltot[p, d] + totals[z, d] for d in range(3)]
    for i in range(1, NR):
        slot = (p + i) & (NR - 1)
        acc = [acc[d] + crs[slot, d] for d in range(3)]
    arrived(group_recv.at[3], rs2.at[pl.ds(0, NZ - 1)])
    for i in range(1, NZ):
        slot = (z + i) & (NZ - 1)
        acc = [acc[d] + rs2[slot, d] for d in range(3)]
    for d in range(3):
        total = strength * acc[d] + own_f[d]
        for b in range(OWN):
            out[d : d + 1, b * BLK : (b + 1) * BLK] = total[b : b + 1, :]
    arrived(sent.at[8], totals.at[pl.ds(0, NZ - 1)])


def on_device(NR, NY, NZ, positions, velocities, chain_order, tile_list):
    f32, i32 = jnp.float32, jnp.int32
    dma = pltpu.SemaphoreType.DMA
    in_hbm = pl.BlockSpec(memory_space=pltpu.HBM)
    forces = pl.pallas_call(
        functools.partial(kernel, NR, NY, NZ),
        out_shape=jax.ShapeDtypeStruct(positions.shape, f32),
        in_specs=[in_hbm] * 3,
        out_specs=pl.BlockSpec(memory_space=pltpu.VMEM),
        scratch_shapes=[
            pltpu.SMEM(tile_list.shape, i32),
            pltpu.VMEM(tile_list.shape, i32),
            pltpu.VMEM(positions.shape, f32),
            pltpu.VMEM((OWN, BLK), i32),
            pltpu.VMEM((NY * NZ, 3, OWN, BLK), f32),
            pltpu.VMEM((NR, 3, OWN, BLK), f32),
            pltpu.VMEM((NY * NZ, 3, OWN, BLK), i32),
            pltpu.VMEM((NR, 3, OWN, BLK), i32),
            pltpu.VMEM((2, 4, 3, 8, BLK), i32),
            pltpu.VMEM((2, 4, 3, 8, BLK), i32),
            pltpu.VMEM((8, 3, 8, BLK), f32),
            pltpu.VMEM((6, 8, BLK), f32),
            pltpu.VMEM((3, OWN, BLK), f32),
            pltpu.VMEM((OWN, BLK), f32),
            pltpu.VMEM((NY, 8, BLK), f32),
            pltpu.VMEM((BATCHES, NY, 3, GROUP, BLK), f32),
            pltpu.VMEM((BATCHES, 3, GROUP, BLK), f32),
            pltpu.VMEM((NZ, 3, OWN, BLK), f32),
            pltpu.VMEM((NR, 3, OWN, BLK), f32),
            pltpu.VMEM((NZ, 3, OWN, BLK), f32),
            pltpu.VMEM((NR, 3, OWN, BLK), f32),
            dma((4,)),
            dma((9,)),
            dma((2, NZ)),
            dma((2, max(NY, NZ))),
            dma((4,)),
            dma((2,)),
        ],
        compiler_params=pltpu.CompilerParams(
            collective_id=0, has_side_effects=True, vmem_limit_bytes=56 * 1024 * 1024
        ),
    )(tile_list, positions, chain_order)
    new_velocity = velocities + time_step * forces
    new_position = positions + time_step * new_velocity
    return (new_velocity, new_position)


def solution(mesh, NZ=8):
    in_specs = (
        P(None, ("row", "col")),
        P(None, ("row", "col")),
        P(("row", "col"), None),
        P(None, ("row", "col")),
    )
    out_specs = (P(None, ("row", "col")), P(None, ("row", "col")))
    return jax.shard_map(
        functools.partial(on_device, mesh.shape["row"], mesh.shape["col"] // NZ, NZ),
        mesh=mesh,
        in_specs=in_specs,
        out_specs=out_specs,
        check_vma=False,
    )
```

```python
import functools

import jax
import jax.numpy as jnp
from jax import lax
from jax.experimental import pallas as pl
from jax.experimental.pallas import tpu as pltpu
from jax.sharding import PartitionSpec as P

BLK = 128
CHAIN = 32
LINES_X = 4
LINES_Y = 4
OWN = 16
FAR = 64
GROUP = 8
BATCHES = FAR // GROUP
MESH = pl.DeviceIdType.MESH

cutoff = 2.5
spacing = 1.1
spring = 30.0
bond_reach = 1.5
time_step = 0.005
shift_force = 24.0 * (2.0 * cutoff ** (-13) - cutoff ** (-7))
strength = -shift_force
unit = (48.0 / strength) ** (1.0 / 13.0)
middle = 0.5 * unit**6


def to_phase(x, period):
    per_unit = 2.0**32 / period
    whole = round(per_unit)
    n = jnp.floor(x)
    rest = n * jnp.float32(per_unit - whole) + (x - n) * jnp.float32(per_unit)
    return n.astype(jnp.int32) * jnp.int32(whole) + rest.astype(jnp.int32)


def pair(row, column, scales, extra=None):
    d = [(a - b).astype(jnp.float32) * s for a, b, s in zip(row, column, scales)]
    squared = d[0] * d[0] + d[1] * d[1] + d[2] * d[2]
    if extra is not None:
        squared = squared + extra
    t = lax.rsqrt(squared)
    s = t * t
    cubed = s * s * s
    magnitude = (s * cubed) * (cubed - jnp.float32(middle)) + t
    magnitude = jnp.where(squared < jnp.float32((cutoff / unit) ** 2), magnitude, 0.0)
    return [v * magnitude for v in d]


def skew(row, first):
    wide = jnp.broadcast_to(row, (8, BLK))
    return pltpu.roll(wide, first, 1, stride=1, stride_axis=0)


def meet(rows, columns, scales, extra, last_mask):
    to_rows = [None] * len(rows)
    to_columns = [None] * len(columns)
    for i, row in enumerate(rows):
        for j, column in enumerate(columns):
            f = pair(row, column, scales, extra if i + j == 0 else None)
            to_rows[i] = f if j == 0 else [x + v for x, v in zip(to_rows[i], f)]
            if last_mask is not None and (i, j) == (len(rows) - 1, len(columns) - 1):
                f = [jnp.where(last_mask, v, 0.0) for v in f]
            to_columns[j] = f if i == 0 else [x + v for x, v in zip(to_columns[j], f)]
    return to_rows, to_columns


def settle_row(parts):
    total = parts[0]
    for i, v in enumerate(parts[1:], 1):
        total = total + pltpu.roll(v, 8 * i, 1)
    return total


def settle_column(parts, shifts):
    total = None
    for v, shift in zip(parts, shifts):
        v = pltpu.roll(v, BLK - shift, 1) if shift else v
        total = v if total is None else total + v
    return total


def unskew(total, index):
    return jnp.take_along_axis(total, index, axis=1, mode="promise_in_bounds")


def fold(total):
    return jnp.sum(total, axis=0, keepdims=True)


FAR_SHIFTS = (0, 32, 64, 96)
SELF_SHIFTS = (1, 17, 33, 49)


def spread(one_hot, parts):
    total = None
    for _ in range(3):
        piece = parts.astype(jnp.bfloat16)
        parts = parts - piece.astype(jnp.float32)
        product = jnp.dot(one_hot, piece, preferred_element_type=jnp.float32)
        total = product if total is None else total + product
    return total


def kernel(
    NR, NY, NZ,
    tl_any, pos_any, chain_any, out,
    tl, tlv, pos, chain, gath, colg, gath_u, colg_u, rowed, skewed, held, rolled,
    own_f, inv, meta, prs, cparts, totals, coltot, rs2, crs,
    in_sem, sent, a_recv, b_recv, group_recv, r1_recv,
):
    periods = [
        4.0 * spacing * LINES_X * NY * NZ,
        4.0 * spacing * LINES_Y * NR,
        8.0 * spacing,
    ]
    scales = [jnp.float32(v / 2.0**32 / unit) for v in periods]
    p = lax.axis_index("row")
    q = lax.axis_index("col")
    y = q >> (NZ.bit_length() - 1)
    z = q & (NZ - 1)

    def at_z(d):
        return (p, y * NZ + ((z + d) & (NZ - 1)))

    def at_y(d):
        return (p, ((y + d) & (NY - 1)) * NZ + z)

    def at_row(d):
        return ((p + d) & (NR - 1), q)

    barrier = pltpu.get_barrier_semaphore()
    peers = (
        [at_z(d) for d in sorted(range(1, NZ), key=lambda d: -min(d, NZ - d))]
        + [at_y(d) for d in range(1, NY)]
        + [at_row(d) for d in range(1, NR)]
    )
    for peer in peers:
        pl.semaphore_signal(barrier, inc=1, device_id=peer, device_id_type=MESH)
    reads = [
        pltpu.make_async_copy(src, dst, in_sem.at[i])
        for i, (src, dst) in enumerate(
            [(pos_any, pos), (chain_any, chain), (tl_any, tl), (tl_any, tlv)]
        )
    ]
    for read in reads:
        read.start()

    y_order = [1, NY - 1] + list(range(2, NY - 1)) if NY > 2 else [1]
    z_order = [(i + 1) // 2 if i % 2 else NZ - i // 2 for i in range(1, NZ)]

    def copy(src, dst, send, recv, peer):
        return pltpu.make_async_remote_copy(
            src_ref=src, dst_ref=dst, send_sem=send, recv_sem=recv,
            device_id=peer, device_id_type=MESH,
        )

    def arrived(sem, like):
        pltpu.make_async_copy(like, like, sem).wait()

    def slot_of(u, v):
        return ((y + u) & (NY - 1)) * NZ + ((z + v) & (NZ - 1))

    def a_part(slot, send, recv, peer):
        ref = gath.at[slot, pl.ds(0, 2)]
        return copy(ref, ref, send, recv, peer)

    def b_part(slot, send, recv, peer):
        ref = gath.at[slot, 2]
        return copy(ref, ref, send, recv, peer)

    def a_first(d):
        return a_part(q, sent.at[0], a_recv.at[0, z], at_z(d))

    def a_then(k, d):
        far_z = (z + k) & (NZ - 1)
        return a_part(y * NZ + far_z, sent.at[1], a_recv.at[1, far_z], at_y(d))

    def b_first(d):
        return b_part(q, sent.at[2], b_recv.at[0, y], at_y(d))

    def b_then(k, d):
        return b_part(((y + k) & (NY - 1)) * NZ + z, sent.at[3], b_recv.at[1, z], at_z(d))

    def row_copy(d):
        return copy(colg.at[p], colg.at[p], sent.at[4], group_recv.at[0], at_row(d))

    def meta_copy(d):
        return copy(meta.at[y], meta.at[y], sent.at[5], group_recv.at[1], at_y(d))

    def a_phase(slot):
        for d in range(2):
            gath_u[slot, d] = to_phase(gath[slot, d], periods[d])

    def b_phase(slot):
        gath_u[slot, 2] = to_phase(gath[slot, 2], periods[2])

    reads[0].wait()
    for b in range(OWN):
        for d in range(3):
            v = pos[d : d + 1, b * BLK : (b + 1) * BLK]
            gath[q, d, b : b + 1, :] = v
            colg[p, d, b : b + 1, :] = v
    lane = lax.broadcasted_iota(jnp.int32, (8, BLK), 1)
    sub = lax.broadcasted_iota(jnp.int32, (8, BLK), 0)
    index = (lane + sub) & (BLK - 1)

    pl.semaphore_wait(barrier, len(peers))
    for d in y_order:
        b_first(d).start()
    for d in z_order[:2]:
        a_first(d).start()
    for d in y_order:
        a_then(0, d).start()
    for d in z_order[2:]:
        a_first(d).start()
    for d in z_order:
        b_then(0, d).start()
    for d in range(1, NR):
        row_copy(d).start()
    for read in reads[1:]:
        read.wait()
    meta[y] = jnp.full((8, BLK), -1.0, jnp.float32)
    meta[y, 0:1, 0:FAR] = tlv[0:1, OWN : OWN + FAR].astype(jnp.float32)

    for d in y_order:
        meta_copy(d).start()

    for d in range(3):
        u = to_phase(gath[q, d], periods[d])
        gath_u[q, d] = u
        colg_u[p, d] = u

    def pass_a(i, carry):
        k = z_step(i)
        slot = slot_of(0, k)
        arrived(a_recv.at[0, (z + k) & (NZ - 1)], gath.at[slot, pl.ds(0, 2)])
        for d in y_order:
            a_then(k, d).start()
        a_phase(slot)
        return carry

    def pass_b(k):
        slot = slot_of(k, 0)
        arrived(b_recv.at[0, (y + k) & (NY - 1)], gath.at[slot, 2])
        for d in reversed(z_order):
            b_then(k, d).start()
        b_phase(slot)

    def z_step(i):
        half = (i >> 1) + 1
        return (half + (i & 1) * (NZ - 2 * half)) & (NZ - 1)

    lax.fori_loop(0, min(2, NZ - 1), pass_a, 0)
    for k in y_order[:2]:
        pass_b(k)
    lax.fori_loop(min(2, NZ - 1), min(4, NZ - 1), pass_a, 0)
    for k in y_order[2:]:
        pass_b(k)
    lax.fori_loop(min(4, NZ - 1), NZ - 1, pass_a, 0)

    arrived(group_recv.at[0], colg.at[pl.ds(0, NR - 1)])
    for i in range(1, NR):
        slot = (p + i) & (NR - 1)
        for d in range(3):
            colg_u[slot, d] = to_phase(colg[slot, d], periods[d])

    def a_rest(k):
        arrived(a_recv.at[1, (z + k) & (NZ - 1)], gath.at[pl.ds(0, NY - 1), pl.ds(0, 2)])
        for d in y_order:
            a_phase(slot_of(d, k))

    def rest(i, carry):
        k = z_step(i)
        arrived(b_recv.at[1, (z + k) & (NZ - 1)], gath.at[pl.ds(0, NY), 2])
        for d in range(NY):
            b_phase(slot_of(d, k))
        a_rest(k)
        return carry

    a_rest(0)
    lax.fori_loop(0, NZ - 1, rest, 0)

    def head(t, rowed, skewed):
        r = tl[0, OWN + t]
        c = tl[1, OWN + t]
        for d in range(3):
            row = jnp.broadcast_to(gath_u[r >> 4, d, pl.ds(r & 15, 1), :], (8, BLK))
            rowed[0, d] = row
            for k in range(1, 4):
                rowed[k, d] = pltpu.roll(row, BLK - 8 * k, 1)
            column = colg_u[c >> 4, d, pl.ds(c & 15, 1), :]
            for k, shift in enumerate(FAR_SHIFTS):
                skewed[k, d] = skew(column, shift)

    def r1_copy(b, d):
        return copy(
            prs.at[b, y], prs.at[b, y], sent.at[6], r1_recv.at[b // (BATCHES - 1)], at_y(d)
        )

    def far_step(t, rowed, skewed, next_rowed, next_skewed):
        before = jnp.maximum(t - 2, 0)
        for d in range(3):
            at = pl.ds(before % GROUP, 1)
            prs[before // GROUP, y, d, at, :] = fold(rolled[d])
            cparts[before // GROUP, d, at, :] = fold(unskew(rolled[3 + d], index))
        for d in range(3):
            rolled[d] = settle_row([held[k, d] for k in range(4)])
            rolled[3 + d] = settle_column([held[4 + k, d] for k in range(4)], FAR_SHIFTS)
        now = jnp.minimum(t, FAR - 1)
        r = tl[0, OWN + now]
        c = tl[1, OWN + now]
        same = p * (NY * NZ * OWN) + r == ((c >> 4) * (NY * NZ) + q) * OWN + (c & 15)
        extra = jnp.where((sub == 0) & same, 1e6, 0.0)
        rows = [[rowed[k, d] for d in range(3)] for k in range(4)]
        columns = [[skewed[k, d] for d in range(3)] for k in range(4)]
        to_rows, to_columns = meet(rows, columns, scales, extra, None)
        head(jnp.minimum(t + 1, FAR - 1), next_rowed, next_skewed)
        for k in range(4):
            for d in range(3):
                held[k, d] = to_rows[k][d]
                held[4 + k, d] = to_columns[k][d]

    def far_steps(i, carry):
        far_step(2 * i, rowed.at[0], skewed.at[0], rowed.at[1], skewed.at[1])
        far_step(2 * i + 1, rowed.at[1], skewed.at[1], rowed.at[0], skewed.at[0])
        return carry

    def batch(b, carry):
        start = b * (GROUP // 2)
        lax.fori_loop(start, start + jnp.where(b < BATCHES, GROUP // 2, 1), far_steps, 0)

        @pl.when(b > 0)
        def _():
            for d in y_order:
                r1_copy(b - 1, d).start()

        return carry

    held[...] = jnp.zeros_like(held)
    rolled[...] = jnp.zeros_like(rolled)
    head(0, rowed.at[0], skewed.at[0])
    lax.fori_loop(0, BATCHES + 1, batch, 0)

    r = tlv[0:1, OWN : OWN + FAR]
    c = tlv[1:2, OWN : OWN + FAR]
    same = p * (NY * NZ * OWN) + r == ((c >> 4) * (NY * NZ) + q) * OWN + (c & 15)
    rows = lax.broadcasted_iota(jnp.int32, (NR * OWN, FAR), 0)
    minus = jnp.where((rows == c) & jnp.logical_not(same), -1.0, 0.0).astype(jnp.bfloat16)
    for d in range(3):
        full = spread(minus, cparts[:, d].reshape(FAR, BLK))
        coltot[:, d] = full.reshape(NR, OWN, BLK)

    def rc_copy(d):
        to = (p + d) & (NR - 1)
        return copy(coltot.at[to], crs.at[p], sent.at[7], group_recv.at[2], at_row(d))

    for d in range(1, NR):
        rc_copy(d).start()

    arrived(sent.at[0], gath.at[pl.ds(0, NZ - 1), pl.ds(0, 2)])
    arrived(sent.at[1], gath.at[pl.ds(0, NZ * (NY - 1)), pl.ds(0, 2)])
    arrived(sent.at[2], gath.at[pl.ds(0, NY - 1), 2])
    arrived(sent.at[3], gath.at[pl.ds(0, NY * (NZ - 1)), 2])
    arrived(sent.at[4], colg.at[pl.ds(0, NR - 1)])
    arrived(sent.at[5], meta.at[pl.ds(0, NY - 1)])

    def self_tile(k):
        u = [gath_u[q, d, pl.ds(k, 1), :] for d in range(3)]
        wide = [jnp.broadcast_to(v, (8, BLK)) for v in u]
        rows = [wide, [pltpu.roll(v, BLK - 8, 1) for v in wide]]
        columns = [[skew(v, shift) for v in u] for shift in SELF_SHIFTS]
        to_rows, to_columns = meet(rows, columns, scales, None, sub < 7)
        for d in range(3):
            force = settle_row([v[d] for v in to_rows])
            force -= unskew(settle_column([v[d] for v in to_columns], SELF_SHIFTS), index)
            own_f[d, pl.ds(k, 1), :] = strength * fold(force)

    def self_tiles(i, carry):
        self_tile(2 * i)
        self_tile(2 * i + 1)
        return carry

    lax.fori_loop(0, OWN // 2, self_tiles, 0)

    arrived(group_recv.at[1], meta.at[pl.ds(0, NY - 1)])

    def chosen(lo, hi):
        names = jnp.concatenate(
            [meta[i, 0:1, b * GROUP : (b + 1) * GROUP] for b in range(lo, hi) for i in range(NY)],
            axis=1,
        )
        count = NY * GROUP * (hi - lo)
        mine = lax.broadcasted_iota(jnp.int32, (NZ * OWN, count), 0) + y * (NZ * OWN)
        return jnp.where(mine.astype(jnp.float32) == names, 1.0, 0.0).astype(jnp.bfloat16)

    last = BATCHES - 1
    early = chosen(0, last)
    late = chosen(last, BATCHES)
    arrived(r1_recv.at[0], prs.at[pl.ds(0, last), pl.ds(0, NY - 1)])
    for d in range(3):
        full = spread(early, prs[0:last, :, d].reshape(last * NY * GROUP, BLK))
        totals[:, d] = full.reshape(NZ, OWN, BLK)
    arrived(r1_recv.at[1], prs.at[last, pl.ds(0, NY - 1)])
    for d in range(3):
        full = spread(late, prs[last, :, d].reshape(NY * GROUP, BLK))
        totals[:, d] += full.reshape(NZ, OWN, BLK)

    def r2_copy(d):
        to = (z + d) & (NZ - 1)
        return copy(totals.at[to], rs2.at[z], sent.at[8], group_recv.at[3], at_z(d))

    for d in reversed(z_order):
        r2_copy(d).start()

    x = [gath[q, d] for d in range(3)]
    order = chain[...]
    order_t = jnp.transpose(order.astype(jnp.float32))
    lane_f = lax.broadcasted_iota(jnp.int32, (BLK, BLK), 1).astype(jnp.float32)
    sub_f = lax.broadcasted_iota(jnp.int32, (BLK, BLK), 0).astype(jnp.float32)
    for b in range(OWN):
        hit = order_t[:, b : b + 1] == lane_f
        inv[b : b + 1, :] = jnp.sum(jnp.where(hit, sub_f, 0.0), axis=0, keepdims=True)
    back = inv[...].astype(jnp.int32)
    ordered = [jnp.take_along_axis(v, order, axis=1, mode="promise_in_bounds") for v in x]
    bond = [pltpu.roll(v, BLK - 1, 1) - v for v in ordered]
    squared = bond[0] * bond[0] + bond[1] * bond[1] + bond[2] * bond[2]
    rank = lax.broadcasted_iota(jnp.int32, (OWN, BLK), 1) + 1
    stiffness = -spring / jnp.maximum(1.0 - squared / (bond_reach * bond_reach), 0.3)
    stiffness = jnp.where(rank % CHAIN != 0, stiffness, 0.0)
    for d in range(3):
        pulled = bond[d] * stiffness
        along = pltpu.roll(pulled, 1, 1) - pulled
        own_f[d] += jnp.take_along_axis(along, back, axis=1, mode="promise_in_bounds")

    arrived(sent.at[6], prs.at[:, pl.ds(0, NY - 1)])
    arrived(sent.at[7], crs.at[pl.ds(0, NR - 1)])
    arrived(group_recv.at[2], crs.at[pl.ds(0, NR - 1)])
    acc = [coltot[p, d] + totals[z, d] for d in range(3)]
    for i in range(1, NR):
        slot = (p + i) & (NR - 1)
        acc = [acc[d] + crs[slot, d] for d in range(3)]
    arrived(group_recv.at[3], rs2.at[pl.ds(0, NZ - 1)])
    for i in range(1, NZ):
        slot = (z + i) & (NZ - 1)
        acc = [acc[d] + rs2[slot, d] for d in range(3)]
    for d in range(3):
        total = strength * acc[d] + own_f[d]
        for b in range(OWN):
            out[d : d + 1, b * BLK : (b + 1) * BLK] = total[b : b + 1, :]
    arrived(sent.at[8], totals.at[pl.ds(0, NZ - 1)])


def on_device(NR, NY, NZ, positions, velocities, chain_order, tile_list):
    f32, i32 = jnp.float32, jnp.int32
    dma = pltpu.SemaphoreType.DMA
    in_hbm = pl.BlockSpec(memory_space=pltpu.HBM)
    forces = pl.pallas_call(
        functools.partial(kernel, NR, NY, NZ),
        out_shape=jax.ShapeDtypeStruct(positions.shape, f32),
        in_specs=[in_hbm] * 3,
        out_specs=pl.BlockSpec(memory_space=pltpu.VMEM),
        scratch_shapes=[
            pltpu.SMEM(tile_list.shape, i32),
            pltpu.VMEM(tile_list.shape, i32),
            pltpu.VMEM(positions.shape, f32),
            pltpu.VMEM((OWN, BLK), i32),
            pltpu.VMEM((NY * NZ, 3, OWN, BLK), f32),
            pltpu.VMEM((NR, 3, OWN, BLK), f32),
            pltpu.VMEM((NY * NZ, 3, OWN, BLK), i32),
            pltpu.VMEM((NR, 3, OWN, BLK), i32),
            pltpu.VMEM((2, 4, 3, 8, BLK), i32),
            pltpu.VMEM((2, 4, 3, 8, BLK), i32),
            pltpu.VMEM((8, 3, 8, BLK), f32),
            pltpu.VMEM((6, 8, BLK), f32),
            pltpu.VMEM((3, OWN, BLK), f32),
            pltpu.VMEM((OWN, BLK), f32),
            pltpu.VMEM((NY, 8, BLK), f32),
            pltpu.VMEM((BATCHES, NY, 3, GROUP, BLK), f32),
            pltpu.VMEM((BATCHES, 3, GROUP, BLK), f32),
            pltpu.VMEM((NZ, 3, OWN, BLK), f32),
            pltpu.VMEM((NR, 3, OWN, BLK), f32),
            pltpu.VMEM((NZ, 3, OWN, BLK), f32),
            pltpu.VMEM((NR, 3, OWN, BLK), f32),
            dma((4,)),
            dma((9,)),
            dma((2, NZ)),
            dma((2, max(NY, NZ))),
            dma((4,)),
            dma((2,)),
        ],
        compiler_params=pltpu.CompilerParams(
            collective_id=0, has_side_effects=True, vmem_limit_bytes=56 * 1024 * 1024
        ),
    )(tile_list, positions, chain_order)
    new_velocity = velocities + time_step * forces
    new_position = positions + time_step * new_velocity
    return (new_velocity, new_position)


def solution(mesh, NZ=8):
    in_specs = (
        P(None, ("row", "col")),
        P(None, ("row", "col")),
        P(("row", "col"), None),
        P(None, ("row", "col")),
    )
    out_specs = (P(None, ("row", "col")), P(None, ("row", "col")))
    return jax.shard_map(
        functools.partial(on_device, mesh.shape["row"], mesh.shape["col"] // NZ, NZ),
        mesh=mesh,
        in_specs=in_specs,
        out_specs=out_specs,
        check_vma=False,
    )
```

```python
import functools

import jax
import jax.numpy as jnp
from jax import lax
from jax.experimental import pallas as pl
from jax.experimental.pallas import tpu as pltpu
from jax.sharding import PartitionSpec as P

BLK = 128
CHAIN = 32
LINES_X = 4
LINES_Y = 4
OWN = 16
FAR = 64
GROUP = 8
BATCHES = FAR // GROUP
MESH = pl.DeviceIdType.MESH

cutoff = 2.5
spacing = 1.1
spring = 30.0
bond_reach = 1.5
time_step = 0.005
shift_force = 24.0 * (2.0 * cutoff ** (-13) - cutoff ** (-7))
strength = -shift_force
unit = (48.0 / strength) ** (1.0 / 13.0)
middle = 0.5 * unit**6


def to_phase(x, period):
    per_unit = 2.0**32 / period
    whole = round(per_unit)
    n = jnp.floor(x)
    rest = n * jnp.float32(per_unit - whole) + (x - n) * jnp.float32(per_unit)
    return n.astype(jnp.int32) * jnp.int32(whole) + rest.astype(jnp.int32)


def pair(row, column, scales, extra=None):
    d = [(a - b).astype(jnp.float32) * s for a, b, s in zip(row, column, scales)]
    squared = d[0] * d[0] + d[1] * d[1] + d[2] * d[2]
    if extra is not None:
        squared = squared + extra
    t = lax.rsqrt(squared)
    s = t * t
    cubed = s * s * s
    magnitude = (s * cubed) * (cubed - jnp.float32(middle)) + t
    magnitude = jnp.where(squared < jnp.float32((cutoff / unit) ** 2), magnitude, 0.0)
    return [v * magnitude for v in d]


def skew(row, first):
    wide = jnp.broadcast_to(row, (8, BLK))
    return pltpu.roll(wide, first, 1, stride=1, stride_axis=0)


def meet(rows, columns, scales, extra, last_mask):
    to_rows = [None] * len(rows)
    to_columns = [None] * len(columns)
    for i, row in enumerate(rows):
        for j, column in enumerate(columns):
            f = pair(row, column, scales, extra if i + j == 0 else None)
            to_rows[i] = f if j == 0 else [x + v for x, v in zip(to_rows[i], f)]
            if last_mask is not None and (i, j) == (len(rows) - 1, len(columns) - 1):
                f = [jnp.where(last_mask, v, 0.0) for v in f]
            to_columns[j] = f if i == 0 else [x + v for x, v in zip(to_columns[j], f)]
    return to_rows, to_columns


def settle_row(parts):
    total = parts[0]
    for i, v in enumerate(parts[1:], 1):
        total = total + pltpu.roll(v, 8 * i, 1)
    return total


def settle_column(parts, shifts):
    total = None
    for v, shift in zip(parts, shifts):
        v = pltpu.roll(v, BLK - shift, 1) if shift else v
        total = v if total is None else total + v
    return total


def unskew(total, index):
    return jnp.take_along_axis(total, index, axis=1, mode="promise_in_bounds")


def fold(total):
    return jnp.sum(total, axis=0, keepdims=True)


FAR_SHIFTS = (0, 32, 64, 96)
SELF_SHIFTS = (1, 17, 33, 49)


def spread(one_hot, parts):
    total = None
    for _ in range(3):
        piece = parts.astype(jnp.bfloat16)
        parts = parts - piece.astype(jnp.float32)
        product = jnp.dot(one_hot, piece, preferred_element_type=jnp.float32)
        total = product if total is None else total + product
    return total


def kernel(
    NR, NY, NZ,
    tl_any, pos_any, chain_any, out,
    tl, tlv, pos, chain, gath, colg, gath_u, colg_u, rowed, skewed, held, rolled,
    own_f, inv, meta, prs, cparts, totals, coltot, rs2, crs,
    in_sem, sent, a_recv, b_recv, group_recv, r1_recv,
):
    periods = [
        4.0 * spacing * LINES_X * NY * NZ,
        4.0 * spacing * LINES_Y * NR,
        8.0 * spacing,
    ]
    scales = [jnp.float32(v / 2.0**32 / unit) for v in periods]
    p = lax.axis_index("row")
    q = lax.axis_index("col")
    y = q >> (NZ.bit_length() - 1)
    z = q & (NZ - 1)

    def at_z(d):
        return (p, y * NZ + ((z + d) & (NZ - 1)))

    def at_y(d):
        return (p, ((y + d) & (NY - 1)) * NZ + z)

    def at_row(d):
        return ((p + d) & (NR - 1), q)

    barrier = pltpu.get_barrier_semaphore()
    peers = (
        [at_z(d) for d in sorted(range(1, NZ), key=lambda d: -min(d, NZ - d))]
        + [at_y(d) for d in range(1, NY)]
        + [at_row(d) for d in range(1, NR)]
    )
    for peer in peers:
        pl.semaphore_signal(barrier, inc=1, device_id=peer, device_id_type=MESH)
    reads = [
        pltpu.make_async_copy(src, dst, in_sem.at[i])
        for i, (src, dst) in enumerate(
            [(pos_any, pos), (chain_any, chain), (tl_any, tl), (tl_any, tlv)]
        )
    ]
    for read in reads:
        read.start()

    y_order = [1, NY - 1] + list(range(2, NY - 1)) if NY > 2 else [1]
    z_order = [(i + 1) // 2 if i % 2 else NZ - i // 2 for i in range(1, NZ)]

    def copy(src, dst, send, recv, peer):
        return pltpu.make_async_remote_copy(
            src_ref=src, dst_ref=dst, send_sem=send, recv_sem=recv,
            device_id=peer, device_id_type=MESH,
        )

    def arrived(sem, like):
        pltpu.make_async_copy(like, like, sem).wait()

    def slot_of(u, v):
        return ((y + u) & (NY - 1)) * NZ + ((z + v) & (NZ - 1))

    def a_part(slot, send, recv, peer):
        ref = gath.at[slot, pl.ds(0, 2)]
        return copy(ref, ref, send, recv, peer)

    def b_part(slot, send, recv, peer):
        ref = gath.at[slot, 2]
        return copy(ref, ref, send, recv, peer)

    def a_first(d):
        return a_part(q, sent.at[0], a_recv.at[0, z], at_z(d))

    def a_then(k, d):
        far_z = (z + k) & (NZ - 1)
        return a_part(y * NZ + far_z, sent.at[1], a_recv.at[1, far_z], at_y(d))

    def b_first(d):
        return b_part(q, sent.at[2], b_recv.at[0, y], at_y(d))

    def b_then(k, d):
        return b_part(((y + k) & (NY - 1)) * NZ + z, sent.at[3], b_recv.at[1, z], at_z(d))

    def row_copy(d):
        return copy(colg.at[p], colg.at[p], sent.at[4], group_recv.at[0], at_row(d))

    def meta_copy(d):
        return copy(meta.at[y], meta.at[y], sent.at[5], group_recv.at[1], at_y(d))

    def a_phase(slot):
        for d in range(2):
            gath_u[slot, d] = to_phase(gath[slot, d], periods[d])

    def b_phase(slot):
        gath_u[slot, 2] = to_phase(gath[slot, 2], periods[2])

    reads[0].wait()
    for b in range(OWN):
        for d in range(3):
            v = pos[d : d + 1, b * BLK : (b + 1) * BLK]
            gath[q, d, b : b + 1, :] = v
            colg[p, d, b : b + 1, :] = v
    lane = lax.broadcasted_iota(jnp.int32, (8, BLK), 1)
    sub = lax.broadcasted_iota(jnp.int32, (8, BLK), 0)
    index = (lane + sub) & (BLK - 1)

    pl.semaphore_wait(barrier, len(peers))
    for d in y_order:
        b_first(d).start()
    for d in z_order[:2]:
        a_first(d).start()
    for d in y_order:
        a_then(0, d).start()
    for d in z_order[2:]:
        a_first(d).start()
    for d in z_order:
        b_then(0, d).start()
    for d in range(1, NR):
        row_copy(d).start()
    for read in reads[1:]:
        read.wait()
    meta[y] = jnp.full((8, BLK), -1.0, jnp.float32)
    meta[y, 0:1, 0:FAR] = tlv[0:1, OWN : OWN + FAR].astype(jnp.float32)

    for d in y_order:
        meta_copy(d).start()

    for d in range(3):
        u = to_phase(gath[q, d], periods[d])
        gath_u[q, d] = u
        colg_u[p, d] = u

    def pass_a(i, carry):
        k = z_step(i)
        slot = slot_of(0, k)
        arrived(a_recv.at[0, (z + k) & (NZ - 1)], gath.at[slot, pl.ds(0, 2)])
        for d in y_order:
            a_then(k, d).start()
        a_phase(slot)
        return carry

    def pass_b(k):
        slot = slot_of(k, 0)
        arrived(b_recv.at[0, (y + k) & (NY - 1)], gath.at[slot, 2])
        for d in reversed(z_order):
            b_then(k, d).start()
        b_phase(slot)

    def z_step(i):
        half = (i >> 1) + 1
        return (half + (i & 1) * (NZ - 2 * half)) & (NZ - 1)

    lax.fori_loop(0, min(2, NZ - 1), pass_a, 0)
    for k in y_order[:2]:
        pass_b(k)
    lax.fori_loop(min(2, NZ - 1), min(4, NZ - 1), pass_a, 0)
    for k in y_order[2:]:
        pass_b(k)
    lax.fori_loop(min(4, NZ - 1), NZ - 1, pass_a, 0)

    arrived(group_recv.at[0], colg.at[pl.ds(0, NR - 1)])
    for i in range(1, NR):
        slot = (p + i) & (NR - 1)
        for d in range(3):
            colg_u[slot, d] = to_phase(colg[slot, d], periods[d])

    def a_rest(k):
        arrived(a_recv.at[1, (z + k) & (NZ - 1)], gath.at[pl.ds(0, NY - 1), pl.ds(0, 2)])
        for d in y_order:
            a_phase(slot_of(d, k))

    def rest(i, carry):
        k = z_step(i)
        arrived(b_recv.at[1, (z + k) & (NZ - 1)], gath.at[pl.ds(0, NY), 2])
        for d in range(NY):
            b_phase(slot_of(d, k))
        a_rest(k)
        return carry

    a_rest(0)
    lax.fori_loop(0, NZ - 1, rest, 0)

    def head(t, rowed, skewed):
        r = tl[0, OWN + t]
        c = tl[1, OWN + t]
        for d in range(3):
            row = jnp.broadcast_to(gath_u[r >> 4, d, pl.ds(r & 15, 1), :], (8, BLK))
            rowed[0, d] = row
            for k in range(1, 4):
                rowed[k, d] = pltpu.roll(row, BLK - 8 * k, 1)
            column = colg_u[c >> 4, d, pl.ds(c & 15, 1), :]
            for k, shift in enumerate(FAR_SHIFTS):
                skewed[k, d] = skew(column, shift)

    def r1_copy(b, d):
        return copy(
            prs.at[b, y], prs.at[b, y], sent.at[6], r1_recv.at[b // (BATCHES - 1)], at_y(d)
        )

    def far_step(t, rowed, skewed, next_rowed, next_skewed):
        head(jnp.minimum(t + 1, FAR - 1), next_rowed, next_skewed)
        before = jnp.maximum(t - 2, 0)
        for d in range(3):
            at = pl.ds(before % GROUP, 1)
            prs[before // GROUP, y, d, at, :] = fold(rolled[d])
            cparts[before // GROUP, d, at, :] = fold(unskew(rolled[3 + d], index))
        for d in range(3):
            rolled[d] = settle_row([held[k, d] for k in range(4)])
            rolled[3 + d] = settle_column([held[4 + k, d] for k in range(4)], FAR_SHIFTS)
        now = jnp.minimum(t, FAR - 1)
        r = tl[0, OWN + now]
        c = tl[1, OWN + now]
        same = p * (NY * NZ * OWN) + r == ((c >> 4) * (NY * NZ) + q) * OWN + (c & 15)
        extra = jnp.where((sub == 0) & same, 1e6, 0.0)
        rows = [[rowed[k, d] for d in range(3)] for k in range(4)]
        columns = [[skewed[k, d] for d in range(3)] for k in range(4)]
        to_rows, to_columns = meet(rows, columns, scales, extra, None)
        for k in range(4):
            for d in range(3):
                held[k, d] = to_rows[k][d]
                held[4 + k, d] = to_columns[k][d]

    def far_steps(i, carry):
        far_step(2 * i, rowed.at[0], skewed.at[0], rowed.at[1], skewed.at[1])
        far_step(2 * i + 1, rowed.at[1], skewed.at[1], rowed.at[0], skewed.at[0])
        return carry

    def batch(b, carry):
        start = b * (GROUP // 2)
        lax.fori_loop(start, start + jnp.where(b < BATCHES, GROUP // 2, 1), far_steps, 0)

        @pl.when(b > 0)
        def _():
            for d in y_order:
                r1_copy(b - 1, d).start()

        return carry

    held[...] = jnp.zeros_like(held)
    rolled[...] = jnp.zeros_like(rolled)
    head(0, rowed.at[0], skewed.at[0])
    lax.fori_loop(0, BATCHES + 1, batch, 0)

    r = tlv[0:1, OWN : OWN + FAR]
    c = tlv[1:2, OWN : OWN + FAR]
    same = p * (NY * NZ * OWN) + r == ((c >> 4) * (NY * NZ) + q) * OWN + (c & 15)
    rows = lax.broadcasted_iota(jnp.int32, (NR * OWN, FAR), 0)
    minus = jnp.where((rows == c) & jnp.logical_not(same), -1.0, 0.0).astype(jnp.bfloat16)
    for d in range(3):
        full = spread(minus, cparts[:, d].reshape(FAR, BLK))
        coltot[:, d] = full.reshape(NR, OWN, BLK)

    def rc_copy(d):
        to = (p + d) & (NR - 1)
        return copy(coltot.at[to], crs.at[p], sent.at[7], group_recv.at[2], at_row(d))

    for d in range(1, NR):
        rc_copy(d).start()

    arrived(sent.at[0], gath.at[pl.ds(0, NZ - 1), pl.ds(0, 2)])
    arrived(sent.at[1], gath.at[pl.ds(0, NZ * (NY - 1)), pl.ds(0, 2)])
    arrived(sent.at[2], gath.at[pl.ds(0, NY - 1), 2])
    arrived(sent.at[3], gath.at[pl.ds(0, NY * (NZ - 1)), 2])
    arrived(sent.at[4], colg.at[pl.ds(0, NR - 1)])
    arrived(sent.at[5], meta.at[pl.ds(0, NY - 1)])

    def self_tile(k):
        u = [gath_u[q, d, pl.ds(k, 1), :] for d in range(3)]
        wide = [jnp.broadcast_to(v, (8, BLK)) for v in u]
        rows = [wide, [pltpu.roll(v, BLK - 8, 1) for v in wide]]
        columns = [[skew(v, shift) for v in u] for shift in SELF_SHIFTS]
        to_rows, to_columns = meet(rows, columns, scales, None, sub < 7)
        for d in range(3):
            force = settle_row([v[d] for v in to_rows])
            force -= unskew(settle_column([v[d] for v in to_columns], SELF_SHIFTS), index)
            own_f[d, pl.ds(k, 1), :] = strength * fold(force)

    def self_tiles(i, carry):
        self_tile(2 * i)
        self_tile(2 * i + 1)
        return carry

    lax.fori_loop(0, OWN // 2, self_tiles, 0)

    arrived(group_recv.at[1], meta.at[pl.ds(0, NY - 1)])

    def chosen(lo, hi):
        names = jnp.concatenate(
            [meta[i, 0:1, b * GROUP : (b + 1) * GROUP] for b in range(lo, hi) for i in range(NY)],
            axis=1,
        )
        count = NY * GROUP * (hi - lo)
        mine = lax.broadcasted_iota(jnp.int32, (NZ * OWN, count), 0) + y * (NZ * OWN)
        return jnp.where(mine.astype(jnp.float32) == names, 1.0, 0.0).astype(jnp.bfloat16)

    last = BATCHES - 1
    early = chosen(0, last)
    late = chosen(last, BATCHES)
    arrived(r1_recv.at[0], prs.at[pl.ds(0, last), pl.ds(0, NY - 1)])
    for d in range(3):
        full = spread(early, prs[0:last, :, d].reshape(last * NY * GROUP, BLK))
        totals[:, d] = full.reshape(NZ, OWN, BLK)
    arrived(r1_recv.at[1], prs.at[last, pl.ds(0, NY - 1)])
    for d in range(3):
        full = spread(late, prs[last, :, d].reshape(NY * GROUP, BLK))
        totals[:, d] += full.reshape(NZ, OWN, BLK)

    def r2_copy(d):
        to = (z + d) & (NZ - 1)
        return copy(totals.at[to], rs2.at[z], sent.at[8], group_recv.at[3], at_z(d))

    for d in reversed(z_order):
        r2_copy(d).start()

    x = [gath[q, d] for d in range(3)]
    order = chain[...]
    order_t = jnp.transpose(order.astype(jnp.float32))
    lane_f = lax.broadcasted_iota(jnp.int32, (BLK, BLK), 1).astype(jnp.float32)
    sub_f = lax.broadcasted_iota(jnp.int32, (BLK, BLK), 0).astype(jnp.float32)
    for b in range(OWN):
        hit = order_t[:, b : b + 1] == lane_f
        inv[b : b + 1, :] = jnp.sum(jnp.where(hit, sub_f, 0.0), axis=0, keepdims=True)
    back = inv[...].astype(jnp.int32)
    ordered = [jnp.take_along_axis(v, order, axis=1, mode="promise_in_bounds") for v in x]
    bond = [pltpu.roll(v, BLK - 1, 1) - v for v in ordered]
    squared = bond[0] * bond[0] + bond[1] * bond[1] + bond[2] * bond[2]
    rank = lax.broadcasted_iota(jnp.int32, (OWN, BLK), 1) + 1
    stiffness = -spring / jnp.maximum(1.0 - squared / (bond_reach * bond_reach), 0.3)
    stiffness = jnp.where(rank % CHAIN != 0, stiffness, 0.0)
    for d in range(3):
        pulled = bond[d] * stiffness
        along = pltpu.roll(pulled, 1, 1) - pulled
        own_f[d] += jnp.take_along_axis(along, back, axis=1, mode="promise_in_bounds")

    arrived(sent.at[6], prs.at[:, pl.ds(0, NY - 1)])
    arrived(sent.at[7], crs.at[pl.ds(0, NR - 1)])
    arrived(group_recv.at[2], crs.at[pl.ds(0, NR - 1)])
    acc = [coltot[p, d] + totals[z, d] for d in range(3)]
    for i in range(1, NR):
        slot = (p + i) & (NR - 1)
        acc = [acc[d] + crs[slot, d] for d in range(3)]
    arrived(group_recv.at[3], rs2.at[pl.ds(0, NZ - 1)])
    for i in range(1, NZ):
        slot = (z + i) & (NZ - 1)
        acc = [acc[d] + rs2[slot, d] for d in range(3)]
    for d in range(3):
        total = strength * acc[d] + own_f[d]
        for b in range(OWN):
            out[d : d + 1, b * BLK : (b + 1) * BLK] = total[b : b + 1, :]
    arrived(sent.at[8], totals.at[pl.ds(0, NZ - 1)])


def on_device(NR, NY, NZ, positions, velocities, chain_order, tile_list):
    f32, i32 = jnp.float32, jnp.int32
    dma = pltpu.SemaphoreType.DMA
    in_hbm = pl.BlockSpec(memory_space=pltpu.HBM)
    forces = pl.pallas_call(
        functools.partial(kernel, NR, NY, NZ),
        out_shape=jax.ShapeDtypeStruct(positions.shape, f32),
        in_specs=[in_hbm] * 3,
        out_specs=pl.BlockSpec(memory_space=pltpu.VMEM),
        scratch_shapes=[
            pltpu.SMEM(tile_list.shape, i32),
            pltpu.VMEM(tile_list.shape, i32),
            pltpu.VMEM(positions.shape, f32),
            pltpu.VMEM((OWN, BLK), i32),
            pltpu.VMEM((NY * NZ, 3, OWN, BLK), f32),
            pltpu.VMEM((NR, 3, OWN, BLK), f32),
            pltpu.VMEM((NY * NZ, 3, OWN, BLK), i32),
            pltpu.VMEM((NR, 3, OWN, BLK), i32),
            pltpu.VMEM((2, 4, 3, 8, BLK), i32),
            pltpu.VMEM((2, 4, 3, 8, BLK), i32),
            pltpu.VMEM((8, 3, 8, BLK), f32),
            pltpu.VMEM((6, 8, BLK), f32),
            pltpu.VMEM((3, OWN, BLK), f32),
            pltpu.VMEM((OWN, BLK), f32),
            pltpu.VMEM((NY, 8, BLK), f32),
            pltpu.VMEM((BATCHES, NY, 3, GROUP, BLK), f32),
            pltpu.VMEM((BATCHES, 3, GROUP, BLK), f32),
            pltpu.VMEM((NZ, 3, OWN, BLK), f32),
            pltpu.VMEM((NR, 3, OWN, BLK), f32),
            pltpu.VMEM((NZ, 3, OWN, BLK), f32),
            pltpu.VMEM((NR, 3, OWN, BLK), f32),
            dma((4,)),
            dma((9,)),
            dma((2, NZ)),
            dma((2, max(NY, NZ))),
            dma((4,)),
            dma((2,)),
        ],
        compiler_params=pltpu.CompilerParams(
            collective_id=0, has_side_effects=True, vmem_limit_bytes=32 * 1024 * 1024
        ),
    )(*[pltpu.with_memory_space_constraint(v, pltpu.HBM) for v in (tile_list, positions, chain_order)])
    new_velocity = velocities + time_step * forces
    new_position = positions + time_step * new_velocity
    return (new_velocity, new_position)


def solution(mesh, NZ=8):
    in_specs = (
        P(None, ("row", "col")),
        P(None, ("row", "col")),
        P(("row", "col"), None),
        P(None, ("row", "col")),
    )
    out_specs = (P(None, ("row", "col")), P(None, ("row", "col")))
    return jax.shard_map(
        functools.partial(on_device, mesh.shape["row"], mesh.shape["col"] // NZ, NZ),
        mesh=mesh,
        in_specs=in_specs,
        out_specs=out_specs,
        check_vma=False,
    )
```

```python
import functools

import jax
import jax.numpy as jnp
from jax import lax
from jax.experimental import pallas as pl
from jax.experimental.pallas import tpu as pltpu
from jax.sharding import PartitionSpec as P

BLK = 128
CHAIN = 32
LINES_X = 4
LINES_Y = 4
OWN = 16
FAR = 64
GROUP = 8
BATCHES = FAR // GROUP
MESH = pl.DeviceIdType.MESH

cutoff = 2.5
spacing = 1.1
spring = 30.0
bond_reach = 1.5
time_step = 0.005
shift_force = 24.0 * (2.0 * cutoff ** (-13) - cutoff ** (-7))
strength = -shift_force
unit = (48.0 / strength) ** (1.0 / 13.0)
middle = 0.5 * unit**6


def to_phase(x, period):
    per_unit = 2.0**32 / period
    whole = round(per_unit)
    n = jnp.floor(x)
    rest = n * jnp.float32(per_unit - whole) + (x - n) * jnp.float32(per_unit)
    return n.astype(jnp.int32) * jnp.int32(whole) + rest.astype(jnp.int32)


def pair(row, column, scales, extra=None):
    d = [(a - b).astype(jnp.float32) * s for a, b, s in zip(row, column, scales)]
    squared = d[0] * d[0] + d[1] * d[1] + d[2] * d[2]
    if extra is not None:
        squared = squared + extra
    t = lax.rsqrt(squared)
    s = t * t
    cubed = s * s * s
    magnitude = (s * cubed) * (cubed - jnp.float32(middle)) + t
    magnitude = jnp.where(squared < jnp.float32((cutoff / unit) ** 2), magnitude, 0.0)
    return [v * magnitude for v in d]


def skew(row, first):
    wide = jnp.broadcast_to(row, (8, BLK))
    return pltpu.roll(wide, first, 1, stride=1, stride_axis=0)


def meet(rows, columns, scales, extra, last_mask):
    to_rows = [None] * len(rows)
    to_columns = [None] * len(columns)
    for i, row in enumerate(rows):
        for j, column in enumerate(columns):
            f = pair(row, column, scales, extra if i + j == 0 else None)
            to_rows[i] = f if j == 0 else [x + v for x, v in zip(to_rows[i], f)]
            if last_mask is not None and (i, j) == (len(rows) - 1, len(columns) - 1):
                f = [jnp.where(last_mask, v, 0.0) for v in f]
            to_columns[j] = f if i == 0 else [x + v for x, v in zip(to_columns[j], f)]
    return to_rows, to_columns


def settle_row(parts):
    total = parts[0]
    for i, v in enumerate(parts[1:], 1):
        total = total + pltpu.roll(v, 8 * i, 1)
    return total


def settle_column(parts, shifts):
    total = None
    for v, shift in zip(parts, shifts):
        v = pltpu.roll(v, BLK - shift, 1) if shift else v
        total = v if total is None else total + v
    return total


def unskew(total, index):
    return jnp.take_along_axis(total, index, axis=1, mode="promise_in_bounds")


def fold(total):
    return jnp.sum(total, axis=0, keepdims=True)


FAR_SHIFTS = (0, 32, 64, 96)
SELF_SHIFTS = (1, 17, 33, 49)


def spread(one_hot, parts):
    total = None
    for _ in range(3):
        piece = parts.astype(jnp.bfloat16)
        parts = parts - piece.astype(jnp.float32)
        product = jnp.dot(one_hot, piece, preferred_element_type=jnp.float32)
        total = product if total is None else total + product
    return total


def kernel(
    NR, NY, NZ,
    tl_any, pos_any, chain_any, out,
    tl, tlv, pos, chain, gath, colg, gath_u, colg_u, rowed, skewed, held, rolled,
    own_f, inv, meta, prs, cparts, totals, coltot, rs2, crs,
    in_sem, sent, a_recv, b_recv, group_recv, r1_recv,
):
    periods = [
        4.0 * spacing * LINES_X * NY * NZ,
        4.0 * spacing * LINES_Y * NR,
        8.0 * spacing,
    ]
    scales = [jnp.float32(v / 2.0**32 / unit) for v in periods]
    p = lax.axis_index("row")
    q = lax.axis_index("col")
    y = q >> (NZ.bit_length() - 1)
    z = q & (NZ - 1)

    def at_z(d):
        return (p, y * NZ + ((z + d) & (NZ - 1)))

    def at_y(d):
        return (p, ((y + d) & (NY - 1)) * NZ + z)

    def at_row(d):
        return ((p + d) & (NR - 1), q)

    barrier = pltpu.get_barrier_semaphore()
    peers = (
        [at_z(d) for d in sorted(range(1, NZ), key=lambda d: -min(d, NZ - d))]
        + [at_y(d) for d in range(1, NY)]
        + [at_row(d) for d in range(1, NR)]
    )
    for peer in peers:
        pl.semaphore_signal(barrier, inc=1, device_id=peer, device_id_type=MESH)
    reads = [
        pltpu.make_async_copy(src, dst, in_sem.at[i])
        for i, (src, dst) in enumerate(
            [(pos_any, pos), (chain_any, chain), (tl_any, tl), (tl_any, tlv)]
        )
    ]
    for read in reads:
        read.start()

    y_order = [1, NY - 1] + list(range(2, NY - 1)) if NY > 2 else [1]
    z_order = [(i + 1) // 2 if i % 2 else NZ - i // 2 for i in range(1, NZ)]

    def copy(src, dst, send, recv, peer):
        return pltpu.make_async_remote_copy(
            src_ref=src, dst_ref=dst, send_sem=send, recv_sem=recv,
            device_id=peer, device_id_type=MESH,
        )

    def arrived(sem, like):
        pltpu.make_async_copy(like, like, sem).wait()

    def slot_of(u, v):
        return ((y + u) & (NY - 1)) * NZ + ((z + v) & (NZ - 1))

    def a_part(slot, send, recv, peer):
        ref = gath.at[slot, pl.ds(0, 2)]
        return copy(ref, ref, send, recv, peer)

    def b_part(slot, send, recv, peer):
        ref = gath.at[slot, 2]
        return copy(ref, ref, send, recv, peer)

    def a_first(d):
        return a_part(q, sent.at[0], a_recv.at[0, z], at_z(d))

    def a_then(k, d):
        far_z = (z + k) & (NZ - 1)
        return a_part(y * NZ + far_z, sent.at[0], a_recv.at[1, far_z], at_y(d))

    def b_first(d):
        return b_part(q, sent.at[1], b_recv.at[y], at_y(d))

    def b_then(k, d):
        return b_part(((y + k) & (NY - 1)) * NZ + z, sent.at[1], a_recv.at[1, z], at_z(d))

    def row_copy(d):
        return copy(colg.at[p], colg.at[p], sent.at[2], group_recv.at[0], at_row(d))

    def meta_copy(d):
        return copy(meta.at[y], meta.at[y], sent.at[3], group_recv.at[1], at_y(d))

    def a_phase(slot):
        for d in range(2):
            gath_u[slot, d] = to_phase(gath[slot, d], periods[d])

    def b_phase(slot):
        gath_u[slot, 2] = to_phase(gath[slot, 2], periods[2])

    reads[0].wait()
    for b in range(OWN):
        for d in range(3):
            v = pos[d : d + 1, b * BLK : (b + 1) * BLK]
            gath[q, d, b : b + 1, :] = v
            colg[p, d, b : b + 1, :] = v
    lane = lax.broadcasted_iota(jnp.int32, (8, BLK), 1)
    sub = lax.broadcasted_iota(jnp.int32, (8, BLK), 0)
    index = (lane + sub) & (BLK - 1)

    pl.semaphore_wait(barrier, len(peers))
    for d in y_order:
        b_first(d).start()
    for d in z_order[:2]:
        a_first(d).start()
    for d in y_order:
        a_then(0, d).start()
    for d in z_order[2:]:
        a_first(d).start()
    for d in range(1, NR):
        row_copy(d).start()
    for d in z_order:
        b_then(0, d).start()
    for read in reads[1:]:
        read.wait()
    meta[y] = jnp.full((8, BLK), -1.0, jnp.float32)
    meta[y, 0:1, 0:FAR] = tlv[0:1, OWN : OWN + FAR].astype(jnp.float32)

    for d in y_order:
        meta_copy(d).start()

    for d in range(3):
        u = to_phase(gath[q, d], periods[d])
        gath_u[q, d] = u
        colg_u[p, d] = u

    def pass_a(i, carry):
        k = z_step(i)
        slot = slot_of(0, k)
        arrived(a_recv.at[0, (z + k) & (NZ - 1)], gath.at[slot, pl.ds(0, 2)])
        for d in y_order:
            a_then(k, d).start()
        a_phase(slot)
        return carry

    def pass_b(k):
        slot = slot_of(k, 0)
        arrived(b_recv.at[(y + k) & (NY - 1)], gath.at[slot, 2])
        for d in reversed(z_order):
            b_then(k, d).start()
        b_phase(slot)

    def z_step(i):
        half = (i >> 1) + 1
        return (half + (i & 1) * (NZ - 2 * half)) & (NZ - 1)

    lax.fori_loop(0, min(2, NZ - 1), pass_a, 0)
    for k in y_order[:2]:
        pass_b(k)
    lax.fori_loop(min(2, NZ - 1), min(4, NZ - 1), pass_a, 0)
    for k in y_order[2:]:
        pass_b(k)
    lax.fori_loop(min(4, NZ - 1), NZ - 1, pass_a, 0)

    arrived(group_recv.at[0], colg.at[pl.ds(0, NR - 1)])
    for i in range(1, NR):
        slot = (p + i) & (NR - 1)
        for d in range(3):
            colg_u[slot, d] = to_phase(colg[slot, d], periods[d])

    def a_rest(k):
        for d in y_order:
            a_phase(slot_of(d, k))

    def rest(i, carry):
        k = z_step(i)
        arrived(a_recv.at[1, (z + k) & (NZ - 1)], gath.at[pl.ds(0, 3 * NY - 2), 2])
        for d in range(NY):
            b_phase(slot_of(d, k))
        a_rest(k)
        return carry

    arrived(a_recv.at[1, z], gath.at[pl.ds(0, NY - 1), pl.ds(0, 2)])
    a_rest(0)
    lax.fori_loop(0, NZ - 1, rest, 0)

    def head(t, rowed, skewed):
        r = tl[0, OWN + t]
        c = tl[1, OWN + t]
        for d in range(3):
            row = jnp.broadcast_to(gath_u[r >> 4, d, pl.ds(r & 15, 1), :], (8, BLK))
            rowed[0, d] = row
            for k in range(1, 4):
                rowed[k, d] = pltpu.roll(row, BLK - 8 * k, 1)
            column = colg_u[c >> 4, d, pl.ds(c & 15, 1), :]
            for k, shift in enumerate(FAR_SHIFTS):
                skewed[k, d] = skew(column, shift)

    def r1_copy(b, d):
        return copy(
            prs.at[b, y], prs.at[b, y], sent.at[4], r1_recv.at[b // (BATCHES - 1)], at_y(d)
        )

    def finish(t):
        for d in range(3):
            at = pl.ds(t % GROUP, 1)
            prs[t // GROUP, y, d, at, :] = fold(rolled[d])
            cparts[t // GROUP, d, at, :] = fold(unskew(rolled[3 + d], index))

    def settle():
        for d in range(3):
            rolled[d] = settle_row([held[k, d] for k in range(4)])
            rolled[3 + d] = settle_column([held[4 + k, d] for k in range(4)], FAR_SHIFTS)

    def far_step(t, rowed, skewed, next_rowed, next_skewed):
        head(jnp.minimum(t + 1, FAR - 1), next_rowed, next_skewed)
        finish(jnp.maximum(t - 2, 0))
        settle()
        r = tl[0, OWN + t]
        c = tl[1, OWN + t]
        same = p * (NY * NZ * OWN) + r == ((c >> 4) * (NY * NZ) + q) * OWN + (c & 15)
        extra = jnp.where((sub == 0) & same, 1e6, 0.0)
        rows = [[rowed[k, d] for d in range(3)] for k in range(4)]
        columns = [[skewed[k, d] for d in range(3)] for k in range(4)]
        to_rows, to_columns = meet(rows, columns, scales, extra, None)
        for k in range(4):
            for d in range(3):
                held[k, d] = to_rows[k][d]
                held[4 + k, d] = to_columns[k][d]

    def far_steps(i, carry):
        far_step(2 * i, rowed.at[0], skewed.at[0], rowed.at[1], skewed.at[1])
        far_step(2 * i + 1, rowed.at[1], skewed.at[1], rowed.at[0], skewed.at[0])
        return carry

    def batch(b, carry):
        start = b * (GROUP // 2)
        lax.fori_loop(start, start + GROUP // 2, far_steps, 0)

        @pl.when(b > 0)
        def _():
            for d in y_order:
                r1_copy(b - 1, d).start()

        return carry

    held[...] = jnp.zeros_like(held)
    rolled[...] = jnp.zeros_like(rolled)
    head(0, rowed.at[0], skewed.at[0])
    lax.fori_loop(0, BATCHES, batch, 0)
    finish(FAR - 2)
    settle()
    finish(FAR - 1)
    for d in reversed(y_order):
        r1_copy(BATCHES - 1, d).start()

    r = tlv[0:1, OWN : OWN + FAR]
    c = tlv[1:2, OWN : OWN + FAR]
    same = p * (NY * NZ * OWN) + r == ((c >> 4) * (NY * NZ) + q) * OWN + (c & 15)
    rows = lax.broadcasted_iota(jnp.int32, (NR * OWN, FAR), 0)
    minus = jnp.where((rows == c) & jnp.logical_not(same), -1.0, 0.0).astype(jnp.bfloat16)
    for d in range(3):
        full = spread(minus, cparts[:, d].reshape(FAR, BLK))
        coltot[:, d] = full.reshape(NR, OWN, BLK)

    def rc_copy(d):
        to = (p + d) & (NR - 1)
        return copy(coltot.at[to], crs.at[p], sent.at[5], group_recv.at[2], at_row(d))

    for d in range(1, NR):
        rc_copy(d).start()

    arrived(sent.at[0], gath.at[pl.ds(0, NY * NZ - 1), pl.ds(0, 2)])
    arrived(sent.at[1], gath.at[pl.ds(0, NY * NZ - 1), 2])
    arrived(sent.at[2], colg.at[pl.ds(0, NR - 1)])
    arrived(sent.at[3], meta.at[pl.ds(0, NY - 1)])

    def self_tile(k):
        u = [gath_u[q, d, pl.ds(k, 1), :] for d in range(3)]
        wide = [jnp.broadcast_to(v, (8, BLK)) for v in u]
        rows = [wide, [pltpu.roll(v, BLK - 8, 1) for v in wide]]
        columns = [[skew(v, shift) for v in u] for shift in SELF_SHIFTS]
        to_rows, to_columns = meet(rows, columns, scales, None, sub < 7)
        for d in range(3):
            force = settle_row([v[d] for v in to_rows])
            force -= unskew(settle_column([v[d] for v in to_columns], SELF_SHIFTS), index)
            own_f[d, pl.ds(k, 1), :] = strength * fold(force)

    def self_tiles(i, carry):
        self_tile(2 * i)
        self_tile(2 * i + 1)
        return carry

    lax.fori_loop(0, OWN // 2, self_tiles, 0)

    arrived(group_recv.at[1], meta.at[pl.ds(0, NY - 1)])

    def chosen(lo, hi):
        names = jnp.concatenate(
            [meta[i, 0:1, b * GROUP : (b + 1) * GROUP] for b in range(lo, hi) for i in range(NY)],
            axis=1,
        )
        count = NY * GROUP * (hi - lo)
        mine = lax.broadcasted_iota(jnp.int32, (NZ * OWN, count), 0) + y * (NZ * OWN)
        return jnp.where(mine.astype(jnp.float32) == names, 1.0, 0.0).astype(jnp.bfloat16)

    last = BATCHES - 1
    early = chosen(0, last)
    late = chosen(last, BATCHES)
    arrived(r1_recv.at[0], prs.at[pl.ds(0, last), pl.ds(0, NY - 1)])
    for d in range(3):
        full = spread(early, prs[0:last, :, d].reshape(last * NY * GROUP, BLK))
        totals[:, d] = full.reshape(NZ, OWN, BLK)
    arrived(r1_recv.at[1], prs.at[last, pl.ds(0, NY - 1)])
    for d in range(3):
        full = spread(late, prs[last, :, d].reshape(NY * GROUP, BLK))
        totals[:, d] += full.reshape(NZ, OWN, BLK)

    def r2_copy(d):
        to = (z + d) & (NZ - 1)
        return copy(totals.at[to], rs2.at[z], sent.at[6], group_recv.at[3], at_z(d))

    for d in reversed(z_order):
        r2_copy(d).start()

    x = [gath[q, d] for d in range(3)]
    order = chain[...]
    order_t = jnp.transpose(order.astype(jnp.float32))
    lane_f = lax.broadcasted_iota(jnp.int32, (BLK, BLK), 1).astype(jnp.float32)
    sub_f = lax.broadcasted_iota(jnp.int32, (BLK, BLK), 0).astype(jnp.float32)
    for b in range(OWN):
        hit = order_t[:, b : b + 1] == lane_f
        inv[b : b + 1, :] = jnp.sum(jnp.where(hit, sub_f, 0.0), axis=0, keepdims=True)
    back = inv[...].astype(jnp.int32)
    ordered = [jnp.take_along_axis(v, order, axis=1, mode="promise_in_bounds") for v in x]
    bond = [pltpu.roll(v, BLK - 1, 1) - v for v in ordered]
    squared = bond[0] * bond[0] + bond[1] * bond[1] + bond[2] * bond[2]
    rank = lax.broadcasted_iota(jnp.int32, (OWN, BLK), 1) + 1
    stiffness = -spring / jnp.maximum(1.0 - squared / (bond_reach * bond_reach), 0.3)
    stiffness = jnp.where(rank % CHAIN != 0, stiffness, 0.0)
    for d in range(3):
        pulled = bond[d] * stiffness
        along = pltpu.roll(pulled, 1, 1) - pulled
        own_f[d] += jnp.take_along_axis(along, back, axis=1, mode="promise_in_bounds")

    arrived(sent.at[4], prs.at[:, pl.ds(0, NY - 1)])
    arrived(sent.at[5], crs.at[pl.ds(0, NR - 1)])
    arrived(group_recv.at[2], crs.at[pl.ds(0, NR - 1)])
    acc = [coltot[p, d] + totals[z, d] for d in range(3)]
    for i in range(1, NR):
        slot = (p + i) & (NR - 1)
        acc = [acc[d] + crs[slot, d] for d in range(3)]
    arrived(group_recv.at[3], rs2.at[pl.ds(0, NZ - 1)])
    for i in range(1, NZ):
        slot = (z + i) & (NZ - 1)
        acc = [acc[d] + rs2[slot, d] for d in range(3)]
    for d in range(3):
        total = strength * acc[d] + own_f[d]
        for b in range(OWN):
            out[d : d + 1, b * BLK : (b + 1) * BLK] = total[b : b + 1, :]
    arrived(sent.at[6], totals.at[pl.ds(0, NZ - 1)])


def on_device(NR, NY, NZ, positions, velocities, chain_order, tile_list):
    f32, i32 = jnp.float32, jnp.int32
    dma = pltpu.SemaphoreType.DMA
    in_hbm = pl.BlockSpec(memory_space=pltpu.HBM)
    forces = pl.pallas_call(
        functools.partial(kernel, NR, NY, NZ),
        out_shape=jax.ShapeDtypeStruct(positions.shape, f32),
        in_specs=[in_hbm] * 3,
        out_specs=pl.BlockSpec(memory_space=pltpu.VMEM),
        scratch_shapes=[
            pltpu.SMEM(tile_list.shape, i32),
            pltpu.VMEM(tile_list.shape, i32),
            pltpu.VMEM(positions.shape, f32),
            pltpu.VMEM((OWN, BLK), i32),
            pltpu.VMEM((NY * NZ, 3, OWN, BLK), f32),
            pltpu.VMEM((NR, 3, OWN, BLK), f32),
            pltpu.VMEM((NY * NZ, 3, OWN, BLK), i32),
            pltpu.VMEM((NR, 3, OWN, BLK), i32),
            pltpu.VMEM((2, 4, 3, 8, BLK), i32),
            pltpu.VMEM((2, 4, 3, 8, BLK), i32),
            pltpu.VMEM((8, 3, 8, BLK), f32),
            pltpu.VMEM((6, 8, BLK), f32),
            pltpu.VMEM((3, OWN, BLK), f32),
            pltpu.VMEM((OWN, BLK), f32),
            pltpu.VMEM((NY, 8, BLK), f32),
            pltpu.VMEM((BATCHES, NY, 3, GROUP, BLK), f32),
            pltpu.VMEM((BATCHES, 3, GROUP, BLK), f32),
            pltpu.VMEM((NZ, 3, OWN, BLK), f32),
            pltpu.VMEM((NR, 3, OWN, BLK), f32),
            pltpu.VMEM((NZ, 3, OWN, BLK), f32),
            pltpu.VMEM((NR, 3, OWN, BLK), f32),
            dma((4,)),
            dma((7,)),
            dma((2, NZ)),
            dma((NY,)),
            dma((4,)),
            dma((2,)),
        ],
        compiler_params=pltpu.CompilerParams(
            collective_id=0, has_side_effects=True, vmem_limit_bytes=32 * 1024 * 1024
        ),
    )(*[pltpu.with_memory_space_constraint(v, pltpu.HBM) for v in (tile_list, positions, chain_order)])
    new_velocity = velocities + time_step * forces
    new_position = positions + time_step * new_velocity
    return (new_velocity, new_position)


def solution(mesh, NZ=8):
    in_specs = (
        P(None, ("row", "col")),
        P(None, ("row", "col")),
        P(("row", "col"), None),
        P(None, ("row", "col")),
    )
    out_specs = (P(None, ("row", "col")), P(None, ("row", "col")))
    return jax.shard_map(
        functools.partial(on_device, mesh.shape["row"], mesh.shape["col"] // NZ, NZ),
        mesh=mesh,
        in_specs=in_specs,
        out_specs=out_specs,
        check_vma=False,
    )
```

```python
import functools

import jax
import jax.numpy as jnp
from jax import lax
from jax.experimental import pallas as pl
from jax.experimental.pallas import tpu as pltpu
from jax.sharding import PartitionSpec as P

BLK = 128
CHAIN = 32
LINES_X = 4
LINES_Y = 4
OWN = 16
FAR = 64
GROUP = 8
BATCHES = FAR // GROUP
MESH = pl.DeviceIdType.MESH

cutoff = 2.5
spacing = 1.1
spring = 30.0
bond_reach = 1.5
time_step = 0.005
shift_force = 24.0 * (2.0 * cutoff ** (-13) - cutoff ** (-7))
strength = -shift_force
unit = (48.0 / strength) ** (1.0 / 13.0)
middle = 0.5 * unit**6


def to_phase(x, period):
    per_unit = 2.0**32 / period
    whole = round(per_unit)
    n = jnp.floor(x)
    rest = n * jnp.float32(per_unit - whole) + (x - n) * jnp.float32(per_unit)
    return n.astype(jnp.int32) * jnp.int32(whole) + rest.astype(jnp.int32)


def pair(row, column, scales, extra=None):
    d = [(a - b).astype(jnp.float32) * s for a, b, s in zip(row, column, scales)]
    squared = d[0] * d[0] + d[1] * d[1] + d[2] * d[2]
    if extra is not None:
        squared = squared + extra
    t = lax.rsqrt(squared)
    s = t * t
    cubed = s * s * s
    magnitude = (s * cubed) * (cubed - jnp.float32(middle)) + t
    magnitude = jnp.where(squared < jnp.float32((cutoff / unit) ** 2), magnitude, 0.0)
    return [v * magnitude for v in d]


def skew(row, first):
    wide = jnp.broadcast_to(row, (8, BLK))
    return pltpu.roll(wide, first, 1, stride=1, stride_axis=0)


def meet(rows, columns, scales, extra, last_mask):
    to_rows = [None] * len(rows)
    to_columns = [None] * len(columns)
    for i, row in enumerate(rows):
        for j, column in enumerate(columns):
            f = pair(row, column, scales, extra if i + j == 0 else None)
            to_rows[i] = f if j == 0 else [x + v for x, v in zip(to_rows[i], f)]
            if last_mask is not None and (i, j) == (len(rows) - 1, len(columns) - 1):
                f = [jnp.where(last_mask, v, 0.0) for v in f]
            to_columns[j] = f if i == 0 else [x + v for x, v in zip(to_columns[j], f)]
    return to_rows, to_columns


def settle_row(parts):
    total = parts[0]
    for i, v in enumerate(parts[1:], 1):
        total = total + pltpu.roll(v, 8 * i, 1)
    return total


def settle_column(parts, shifts):
    total = None
    for v, shift in zip(parts, shifts):
        v = pltpu.roll(v, BLK - shift, 1) if shift else v
        total = v if total is None else total + v
    return total


def unskew(total, index):
    return jnp.take_along_axis(total, index, axis=1, mode="promise_in_bounds")


def fold(total):
    return jnp.sum(total, axis=0, keepdims=True)


FAR_SHIFTS = (0, 32, 64, 96)
SELF_SHIFTS = (1, 17, 33, 49)


def spread(one_hot, parts):
    total = None
    for _ in range(3):
        piece = parts.astype(jnp.bfloat16)
        parts = parts - piece.astype(jnp.float32)
        product = jnp.dot(one_hot, piece, preferred_element_type=jnp.float32)
        total = product if total is None else total + product
    return total


def kernel(
    NR, NY, NZ,
    tl_any, pos_any, chain_any, out,
    tl, tlv, pos, chain, gath, colg, gath_u, colg_u, rowed, skewed, held, rolled,
    own_f, inv, meta, prs, cparts, totals, coltot, rs2, crs,
    in_sem, sent, a_recv, b_recv, group_recv, r1_recv,
):
    periods = [
        4.0 * spacing * LINES_X * NY * NZ,
        4.0 * spacing * LINES_Y * NR,
        8.0 * spacing,
    ]
    scales = [jnp.float32(v / 2.0**32 / unit) for v in periods]
    p = lax.axis_index("row")
    q = lax.axis_index("col")
    y = q >> (NZ.bit_length() - 1)
    z = q & (NZ - 1)

    def at_z(d):
        return (p, y * NZ + ((z + d) & (NZ - 1)))

    def at_y(d):
        return (p, ((y + d) & (NY - 1)) * NZ + z)

    def at_row(d):
        return ((p + d) & (NR - 1), q)

    barrier = pltpu.get_barrier_semaphore()
    peers = (
        [at_z(d) for d in sorted(range(1, NZ), key=lambda d: -min(d, NZ - d))]
        + [at_y(d) for d in range(1, NY)]
        + [at_row(d) for d in range(1, NR)]
    )
    for peer in peers:
        pl.semaphore_signal(barrier, inc=1, device_id=peer, device_id_type=MESH)
    reads = [
        pltpu.make_async_copy(src, dst, in_sem.at[i])
        for i, (src, dst) in enumerate(
            [(pos_any, pos), (chain_any, chain), (tl_any, tl), (tl_any, tlv)]
        )
    ]
    for read in reads:
        read.start()

    y_order = [1, NY - 1] + list(range(2, NY - 1)) if NY > 2 else [1]
    z_order = [(i + 1) // 2 if i % 2 else NZ - i // 2 for i in range(1, NZ)]

    def copy(src, dst, send, recv, peer):
        return pltpu.make_async_remote_copy(
            src_ref=src, dst_ref=dst, send_sem=send, recv_sem=recv,
            device_id=peer, device_id_type=MESH,
        )

    def arrived(sem, like):
        pltpu.make_async_copy(like, like, sem).wait()

    def slot_of(u, v):
        return ((y + u) & (NY - 1)) * NZ + ((z + v) & (NZ - 1))

    def a_part(slot, send, recv, peer):
        ref = gath.at[slot, pl.ds(0, 2)]
        return copy(ref, ref, send, recv, peer)

    def b_part(slot, send, recv, peer):
        ref = gath.at[slot, 2]
        return copy(ref, ref, send, recv, peer)

    def a_first(d):
        return a_part(q, sent.at[0], a_recv.at[0, z], at_z(d))

    def a_then(k, d):
        far_z = (z + k) & (NZ - 1)
        return a_part(y * NZ + far_z, sent.at[0], a_recv.at[1, far_z], at_y(d))

    def b_first(d):
        return b_part(q, sent.at[1], b_recv.at[y], at_y(d))

    def b_then(k, d):
        return b_part(((y + k) & (NY - 1)) * NZ + z, sent.at[1], a_recv.at[1, z], at_z(d))

    def row_copy(d):
        return copy(colg.at[p], colg.at[p], sent.at[2], group_recv.at[0], at_row(d))

    def meta_copy(d):
        return copy(meta.at[y], meta.at[y], sent.at[3], group_recv.at[1], at_y(d))

    def a_phase(slot):
        for d in range(2):
            gath_u[slot, d] = to_phase(gath[slot, d], periods[d])

    def b_phase(slot):
        gath_u[slot, 2] = to_phase(gath[slot, 2], periods[2])

    reads[0].wait()
    for b in range(OWN):
        for d in range(3):
            v = pos[d : d + 1, b * BLK : (b + 1) * BLK]
            gath[q, d, b : b + 1, :] = v
            colg[p, d, b : b + 1, :] = v
    lane = lax.broadcasted_iota(jnp.int32, (8, BLK), 1)
    sub = lax.broadcasted_iota(jnp.int32, (8, BLK), 0)
    index = (lane + sub) & (BLK - 1)

    pl.semaphore_wait(barrier, len(peers))
    for d in z_order:
        a_first(d).start()
    for d in y_order:
        b_first(d).start()
    for d in y_order:
        a_then(0, d).start()
    for d in range(1, NR):
        row_copy(d).start()
    for d in z_order:
        b_then(0, d).start()
    for read in reads[1:]:
        read.wait()
    meta[y] = jnp.full((8, BLK), -1.0, jnp.float32)
    meta[y, 0:1, 0:FAR] = tlv[0:1, OWN : OWN + FAR].astype(jnp.float32)

    for d in y_order:
        meta_copy(d).start()

    for d in range(3):
        u = to_phase(gath[q, d], periods[d])
        gath_u[q, d] = u
        colg_u[p, d] = u

    def pass_a(i, carry):
        k = z_step(i)
        slot = slot_of(0, k)
        arrived(a_recv.at[0, (z + k) & (NZ - 1)], gath.at[slot, pl.ds(0, 2)])
        for d in y_order:
            a_then(k, d).start()
        a_phase(slot)
        return carry

    def pass_b(k):
        slot = slot_of(k, 0)
        arrived(b_recv.at[(y + k) & (NY - 1)], gath.at[slot, 2])
        for d in reversed(z_order):
            b_then(k, d).start()
        b_phase(slot)

    def z_step(i):
        half = (i >> 1) + 1
        return (half + (i & 1) * (NZ - 2 * half)) & (NZ - 1)

    lax.fori_loop(0, min(2, NZ - 1), pass_a, 0)
    for k in y_order[:2]:
        pass_b(k)
    lax.fori_loop(min(2, NZ - 1), min(4, NZ - 1), pass_a, 0)
    for k in y_order[2:]:
        pass_b(k)
    lax.fori_loop(min(4, NZ - 1), NZ - 1, pass_a, 0)

    held[...] = jnp.zeros_like(held)
    rolled[...] = jnp.zeros_like(rolled)
    arrived(group_recv.at[0], colg.at[pl.ds(0, NR - 1)])
    for i in range(1, NR):
        slot = (p + i) & (NR - 1)
        for d in range(3):
            colg_u[slot, d] = to_phase(colg[slot, d], periods[d])

    def a_rest(k):
        for d in y_order:
            a_phase(slot_of(d, k))

    def rest(i, carry):
        k = z_step(i)
        arrived(a_recv.at[1, (z + k) & (NZ - 1)], gath.at[pl.ds(0, 3 * NY - 2), 2])
        for d in range(NY):
            b_phase(slot_of(d, k))
        a_rest(k)
        return carry

    arrived(a_recv.at[1, z], gath.at[pl.ds(0, NY - 1), pl.ds(0, 2)])
    a_rest(0)
    lax.fori_loop(0, NZ - 1, rest, 0)

    def head(t, rowed, skewed):
        r = tl[0, OWN + t]
        c = tl[1, OWN + t]
        for d in range(3):
            row = jnp.broadcast_to(gath_u[r >> 4, d, pl.ds(r & 15, 1), :], (8, BLK))
            rowed[0, d] = row
            for k in range(1, 4):
                rowed[k, d] = pltpu.roll(row, BLK - 8 * k, 1)
            column = colg_u[c >> 4, d, pl.ds(c & 15, 1), :]
            for k, shift in enumerate(FAR_SHIFTS):
                skewed[k, d] = skew(column, shift)

    def r1_copy(b, d):
        return copy(
            prs.at[b, y], prs.at[b, y], sent.at[4], r1_recv.at[b // (BATCHES - 1)], at_y(d)
        )

    def finish(t):
        for d in range(3):
            at = pl.ds(t % GROUP, 1)
            prs[t // GROUP, y, d, at, :] = fold(rolled[d])
            cparts[t // GROUP, d, at, :] = fold(unskew(rolled[3 + d], index))

    def settle():
        for d in range(3):
            rolled[d] = settle_row([held[k, d] for k in range(4)])
            rolled[3 + d] = settle_column([held[4 + k, d] for k in range(4)], FAR_SHIFTS)

    def far_step(t, rowed, skewed, next_rowed, next_skewed):
        head(jnp.minimum(t + 1, FAR - 1), next_rowed, next_skewed)
        finish(jnp.maximum(t - 2, 0))
        settle()
        r = tl[0, OWN + t]
        c = tl[1, OWN + t]
        same = p * (NY * NZ * OWN) + r == ((c >> 4) * (NY * NZ) + q) * OWN + (c & 15)
        extra = jnp.where((sub == 0) & same, 1e6, 0.0)
        rows = [[rowed[k, d] for d in range(3)] for k in range(4)]
        columns = [[skewed[k, d] for d in range(3)] for k in range(4)]
        to_rows, to_columns = meet(rows, columns, scales, extra, None)
        for k in range(4):
            for d in range(3):
                held[k, d] = to_rows[k][d]
                held[4 + k, d] = to_columns[k][d]

    def far_steps(i, carry):
        far_step(2 * i, rowed.at[0], skewed.at[0], rowed.at[1], skewed.at[1])
        far_step(2 * i + 1, rowed.at[1], skewed.at[1], rowed.at[0], skewed.at[0])
        return carry

    def batch(b, carry):
        start = b * (GROUP // 2)
        lax.fori_loop(start, start + GROUP // 2, far_steps, 0)

        @pl.when(b > 0)
        def _():
            for d in y_order:
                r1_copy(b - 1, d).start()

        return carry

    head(0, rowed.at[0], skewed.at[0])
    lax.fori_loop(0, BATCHES, batch, 0)
    finish(FAR - 2)
    settle()
    finish(FAR - 1)
    for d in reversed(y_order):
        r1_copy(BATCHES - 1, d).start()

    r = tlv[0:1, OWN : OWN + FAR]
    c = tlv[1:2, OWN : OWN + FAR]
    same = p * (NY * NZ * OWN) + r == ((c >> 4) * (NY * NZ) + q) * OWN + (c & 15)
    rows = lax.broadcasted_iota(jnp.int32, (NR * OWN, FAR), 0)
    minus = jnp.where((rows == c) & jnp.logical_not(same), -1.0, 0.0).astype(jnp.bfloat16)
    for d in range(3):
        full = spread(minus, cparts[:, d].reshape(FAR, BLK))
        coltot[:, d] = full.reshape(NR, OWN, BLK)

    def rc_copy(d):
        to = (p + d) & (NR - 1)
        return copy(coltot.at[to], crs.at[p], sent.at[5], group_recv.at[2], at_row(d))

    for d in range(1, NR):
        rc_copy(d).start()

    arrived(sent.at[0], gath.at[pl.ds(0, NY * NZ - 1), pl.ds(0, 2)])
    arrived(sent.at[1], gath.at[pl.ds(0, NY * NZ - 1), 2])
    arrived(sent.at[2], colg.at[pl.ds(0, NR - 1)])
    arrived(sent.at[3], meta.at[pl.ds(0, NY - 1)])

    def self_tile(k):
        u = [gath_u[q, d, pl.ds(k, 1), :] for d in range(3)]
        wide = [jnp.broadcast_to(v, (8, BLK)) for v in u]
        rows = [wide, [pltpu.roll(v, BLK - 8, 1) for v in wide]]
        columns = [[skew(v, shift) for v in u] for shift in SELF_SHIFTS]
        to_rows, to_columns = meet(rows, columns, scales, None, sub < 7)
        for d in range(3):
            force = settle_row([v[d] for v in to_rows])
            force -= unskew(settle_column([v[d] for v in to_columns], SELF_SHIFTS), index)
            own_f[d, pl.ds(k, 1), :] = strength * fold(force)

    def self_tiles(i, carry):
        self_tile(2 * i)
        self_tile(2 * i + 1)
        return carry

    lax.fori_loop(0, OWN // 2, self_tiles, 0)

    arrived(group_recv.at[1], meta.at[pl.ds(0, NY - 1)])

    def chosen(lo, hi):
        names = jnp.concatenate(
            [meta[i, 0:1, b * GROUP : (b + 1) * GROUP] for b in range(lo, hi) for i in range(NY)],
            axis=1,
        )
        count = NY * GROUP * (hi - lo)
        mine = lax.broadcasted_iota(jnp.int32, (NZ * OWN, count), 0) + y * (NZ * OWN)
        return jnp.where(mine.astype(jnp.float32) == names, 1.0, 0.0).astype(jnp.bfloat16)

    last = BATCHES - 1
    early = chosen(0, last)
    late = chosen(last, BATCHES)
    arrived(r1_recv.at[0], prs.at[pl.ds(0, last), pl.ds(0, NY - 1)])
    for d in range(3):
        full = spread(early, prs[0:last, :, d].reshape(last * NY * GROUP, BLK))
        totals[:, d] = full.reshape(NZ, OWN, BLK)
    arrived(r1_recv.at[1], prs.at[last, pl.ds(0, NY - 1)])
    for d in range(3):
        full = spread(late, prs[last, :, d].reshape(NY * GROUP, BLK))
        totals[:, d] += full.reshape(NZ, OWN, BLK)

    def r2_copy(d):
        to = (z + d) & (NZ - 1)
        return copy(totals.at[to], rs2.at[z], sent.at[6], group_recv.at[3], at_z(d))

    for d in reversed(z_order):
        r2_copy(d).start()

    x = [gath[q, d] for d in range(3)]
    order = chain[...]
    order_t = jnp.transpose(order.astype(jnp.float32))
    lane_f = lax.broadcasted_iota(jnp.int32, (BLK, BLK), 1).astype(jnp.float32)
    sub_f = lax.broadcasted_iota(jnp.int32, (BLK, BLK), 0).astype(jnp.float32)
    for b in range(OWN):
        hit = order_t[:, b : b + 1] == lane_f
        inv[b : b + 1, :] = jnp.sum(jnp.where(hit, sub_f, 0.0), axis=0, keepdims=True)
    back = inv[...].astype(jnp.int32)
    ordered = [jnp.take_along_axis(v, order, axis=1, mode="promise_in_bounds") for v in x]
    bond = [pltpu.roll(v, BLK - 1, 1) - v for v in ordered]
    squared = bond[0] * bond[0] + bond[1] * bond[1] + bond[2] * bond[2]
    rank = lax.broadcasted_iota(jnp.int32, (OWN, BLK), 1) + 1
    stiffness = -spring / jnp.maximum(1.0 - squared / (bond_reach * bond_reach), 0.3)
    stiffness = jnp.where(rank % CHAIN != 0, stiffness, 0.0)
    for d in range(3):
        pulled = bond[d] * stiffness
        along = pltpu.roll(pulled, 1, 1) - pulled
        own_f[d] += jnp.take_along_axis(along, back, axis=1, mode="promise_in_bounds")

    arrived(sent.at[4], prs.at[:, pl.ds(0, NY - 1)])
    arrived(sent.at[5], crs.at[pl.ds(0, NR - 1)])
    arrived(group_recv.at[2], crs.at[pl.ds(0, NR - 1)])
    acc = [coltot[p, d] + totals[z, d] for d in range(3)]
    for i in range(1, NR):
        slot = (p + i) & (NR - 1)
        acc = [acc[d] + crs[slot, d] for d in range(3)]
    arrived(group_recv.at[3], rs2.at[pl.ds(0, NZ - 1)])
    for i in range(1, NZ):
        slot = (z + i) & (NZ - 1)
        acc = [acc[d] + rs2[slot, d] for d in range(3)]
    for d in range(3):
        total = strength * acc[d] + own_f[d]
        for b in range(OWN):
            out[d : d + 1, b * BLK : (b + 1) * BLK] = total[b : b + 1, :]
    arrived(sent.at[6], totals.at[pl.ds(0, NZ - 1)])


def on_device(NR, NY, NZ, positions, velocities, chain_order, tile_list):
    f32, i32 = jnp.float32, jnp.int32
    dma = pltpu.SemaphoreType.DMA
    in_hbm = pl.BlockSpec(memory_space=pltpu.HBM)
    forces = pl.pallas_call(
        functools.partial(kernel, NR, NY, NZ),
        out_shape=jax.ShapeDtypeStruct(positions.shape, f32),
        in_specs=[in_hbm] * 3,
        out_specs=pl.BlockSpec(memory_space=pltpu.VMEM),
        scratch_shapes=[
            pltpu.SMEM(tile_list.shape, i32),
            pltpu.VMEM(tile_list.shape, i32),
            pltpu.VMEM(positions.shape, f32),
            pltpu.VMEM((OWN, BLK), i32),
            pltpu.VMEM((NY * NZ, 3, OWN, BLK), f32),
            pltpu.VMEM((NR, 3, OWN, BLK), f32),
            pltpu.VMEM((NY * NZ, 3, OWN, BLK), i32),
            pltpu.VMEM((NR, 3, OWN, BLK), i32),
            pltpu.VMEM((2, 4, 3, 8, BLK), i32),
            pltpu.VMEM((2, 4, 3, 8, BLK), i32),
            pltpu.VMEM((8, 3, 8, BLK), f32),
            pltpu.VMEM((6, 8, BLK), f32),
            pltpu.VMEM((3, OWN, BLK), f32),
            pltpu.VMEM((OWN, BLK), f32),
            pltpu.VMEM((NY, 8, BLK), f32),
            pltpu.VMEM((BATCHES, NY, 3, GROUP, BLK), f32),
            pltpu.VMEM((BATCHES, 3, GROUP, BLK), f32),
            pltpu.VMEM((NZ, 3, OWN, BLK), f32),
            pltpu.VMEM((NR, 3, OWN, BLK), f32),
            pltpu.VMEM((NZ, 3, OWN, BLK), f32),
            pltpu.VMEM((NR, 3, OWN, BLK), f32),
            dma((4,)),
            dma((7,)),
            dma((2, NZ)),
            dma((NY,)),
            dma((4,)),
            dma((2,)),
        ],
        compiler_params=pltpu.CompilerParams(
            collective_id=0, has_side_effects=True, vmem_limit_bytes=32 * 1024 * 1024
        ),
    )(*[pltpu.with_memory_space_constraint(v, pltpu.HBM) for v in (tile_list, positions, chain_order)])
    new_velocity = velocities + time_step * forces
    new_position = positions + time_step * new_velocity
    return (new_velocity, new_position)


def solution(mesh, NZ=8):
    in_specs = (
        P(None, ("row", "col")),
        P(None, ("row", "col")),
        P(("row", "col"), None),
        P(None, ("row", "col")),
    )
    out_specs = (P(None, ("row", "col")), P(None, ("row", "col")))
    return jax.shard_map(
        functools.partial(on_device, mesh.shape["row"], mesh.shape["col"] // NZ, NZ),
        mesh=mesh,
        in_specs=in_specs,
        out_specs=out_specs,
        check_vma=False,
    )
```

```python
import functools

import jax
import jax.numpy as jnp
from jax import lax
from jax.experimental import pallas as pl
from jax.experimental.pallas import tpu as pltpu
from jax.sharding import PartitionSpec as P

BLK = 128
CHAIN = 32
LINES_X = 4
LINES_Y = 4
OWN = 16
FAR = 64
GROUP = 8
BATCHES = FAR // GROUP
MESH = pl.DeviceIdType.MESH

cutoff = 2.5
spacing = 1.1
spring = 30.0
bond_reach = 1.5
time_step = 0.005
shift_force = 24.0 * (2.0 * cutoff ** (-13) - cutoff ** (-7))
strength = -shift_force
unit = (48.0 / strength) ** (1.0 / 13.0)
middle = 0.5 * unit**6


def to_phase(x, period):
    per_unit = 2.0**32 / period
    whole = round(per_unit)
    n = jnp.floor(x)
    rest = n * jnp.float32(per_unit - whole) + (x - n) * jnp.float32(per_unit)
    return n.astype(jnp.int32) * jnp.int32(whole) + rest.astype(jnp.int32)


def pair(row, column, scales, extra=None):
    d = [(a - b).astype(jnp.float32) * s for a, b, s in zip(row, column, scales)]
    squared = d[0] * d[0] + d[1] * d[1] + d[2] * d[2]
    if extra is not None:
        squared = squared + extra
    t = lax.rsqrt(squared)
    s = t * t
    cubed = s * s * s
    magnitude = (s * cubed) * (cubed - jnp.float32(middle)) + t
    magnitude = jnp.where(squared < jnp.float32((cutoff / unit) ** 2), magnitude, 0.0)
    return [v * magnitude for v in d]


def skew(row, first):
    wide = jnp.broadcast_to(row, (8, BLK))
    return pltpu.roll(wide, first, 1, stride=1, stride_axis=0)


def meet(rows, columns, scales, extra, last_mask):
    to_rows = [None] * len(rows)
    to_columns = [None] * len(columns)
    for i, row in enumerate(rows):
        for j, column in enumerate(columns):
            f = pair(row, column, scales, extra if i + j == 0 else None)
            to_rows[i] = f if j == 0 else [x + v for x, v in zip(to_rows[i], f)]
            if last_mask is not None and (i, j) == (len(rows) - 1, len(columns) - 1):
                f = [jnp.where(last_mask, v, 0.0) for v in f]
            to_columns[j] = f if i == 0 else [x + v for x, v in zip(to_columns[j], f)]
    return to_rows, to_columns


def settle_row(parts):
    total = parts[0]
    for i, v in enumerate(parts[1:], 1):
        total = total + pltpu.roll(v, 8 * i, 1)
    return total


def settle_column(parts, shifts):
    total = None
    for v, shift in zip(parts, shifts):
        v = pltpu.roll(v, BLK - shift, 1) if shift else v
        total = v if total is None else total + v
    return total


def unskew(total, index):
    return jnp.take_along_axis(total, index, axis=1, mode="promise_in_bounds")


def fold(total):
    return jnp.sum(total, axis=0, keepdims=True)


FAR_SHIFTS = (0, 32, 64, 96)
SELF_SHIFTS = (1, 17, 33, 49)


def spread(one_hot, parts):
    total = None
    for _ in range(3):
        piece = parts.astype(jnp.bfloat16)
        parts = parts - piece.astype(jnp.float32)
        product = jnp.dot(one_hot, piece, preferred_element_type=jnp.float32)
        total = product if total is None else total + product
    return total


def kernel(
    NR, NY, NZ,
    tl_any, pos_any, chain_any, out,
    tl, tlv, pos, chain, gath, colg, gath_u, colg_u, rowed, skewed, held, rolled,
    own_f, inv, meta, prs, cparts, totals, coltot, rs2, crs,
    in_sem, sent, a_recv, b_recv, group_recv, r1_recv,
):
    periods = [
        4.0 * spacing * LINES_X * NY * NZ,
        4.0 * spacing * LINES_Y * NR,
        8.0 * spacing,
    ]
    scales = [jnp.float32(v / 2.0**32 / unit) for v in periods]
    p = lax.axis_index("row")
    q = lax.axis_index("col")
    y = q >> (NZ.bit_length() - 1)
    z = q & (NZ - 1)

    def at_z(d):
        return (p, y * NZ + ((z + d) & (NZ - 1)))

    def at_y(d):
        return (p, ((y + d) & (NY - 1)) * NZ + z)

    def at_row(d):
        return ((p + d) & (NR - 1), q)

    barrier = pltpu.get_barrier_semaphore()
    peers = (
        [at_z(d) for d in sorted(range(1, NZ), key=lambda d: -min(d, NZ - d))]
        + [at_y(d) for d in range(1, NY)]
        + [at_row(d) for d in range(1, NR)]
    )
    for peer in peers:
        pl.semaphore_signal(barrier, inc=1, device_id=peer, device_id_type=MESH)
    reads = [
        pltpu.make_async_copy(src, dst, in_sem.at[i])
        for i, (src, dst) in enumerate(
            [(pos_any, pos), (chain_any, chain), (tl_any, tl), (tl_any, tlv)]
        )
    ]
    for read in reads:
        read.start()

    y_order = [1, NY - 1] + list(range(2, NY - 1)) if NY > 2 else [1]
    z_order = [(i + 1) // 2 if i % 2 else NZ - i // 2 for i in range(1, NZ)]

    def copy(src, dst, send, recv, peer):
        return pltpu.make_async_remote_copy(
            src_ref=src, dst_ref=dst, send_sem=send, recv_sem=recv,
            device_id=peer, device_id_type=MESH,
        )

    def arrived(sem, like):
        pltpu.make_async_copy(like, like, sem).wait()

    def slot_of(u, v):
        return ((y + u) & (NY - 1)) * NZ + ((z + v) & (NZ - 1))

    def a_part(slot, send, recv, peer):
        ref = gath.at[slot, pl.ds(0, 2)]
        return copy(ref, ref, send, recv, peer)

    def b_part(slot, send, recv, peer):
        ref = gath.at[slot, 2]
        return copy(ref, ref, send, recv, peer)

    def a_first(d):
        return a_part(q, sent.at[0], a_recv.at[0, z], at_z(d))

    def a_then(k, d):
        far_z = (z + k) & (NZ - 1)
        return a_part(y * NZ + far_z, sent.at[0], a_recv.at[1, far_z], at_y(d))

    def b_first(d):
        return b_part(q, sent.at[1], b_recv.at[y], at_y(d))

    def b_then(k, d):
        return b_part(((y + k) & (NY - 1)) * NZ + z, sent.at[1], a_recv.at[1, z], at_z(d))

    def row_copy(d):
        return copy(colg.at[p], colg.at[p], sent.at[2], group_recv.at[0], at_row(d))

    def meta_copy(d):
        return copy(meta.at[y], meta.at[y], sent.at[3], group_recv.at[1], at_y(d))

    def a_phase(slot):
        for d in range(2):
            gath_u[slot, d] = to_phase(gath[slot, d], periods[d])

    def b_phase(slot):
        gath_u[slot, 2] = to_phase(gath[slot, 2], periods[2])

    reads[0].wait()
    for b in range(OWN):
        for d in range(3):
            v = pos[d : d + 1, b * BLK : (b + 1) * BLK]
            gath[q, d, b : b + 1, :] = v
            colg[p, d, b : b + 1, :] = v
    lane = lax.broadcasted_iota(jnp.int32, (8, BLK), 1)
    sub = lax.broadcasted_iota(jnp.int32, (8, BLK), 0)
    index = (lane + sub) & (BLK - 1)

    pl.semaphore_wait(barrier, len(peers))
    for d in y_order:
        b_first(d).start()
    for d in z_order:
        a_first(d).start()
    for d in y_order:
        a_then(0, d).start()
    for d in range(1, NR):
        row_copy(d).start()
    for d in z_order:
        b_then(0, d).start()
    for read in reads[1:]:
        read.wait()
    meta[y] = jnp.full((8, BLK), -1.0, jnp.float32)
    meta[y, 0:1, 0:FAR] = tlv[0:1, OWN : OWN + FAR].astype(jnp.float32)

    for d in y_order:
        meta_copy(d).start()

    for d in range(3):
        u = to_phase(gath[q, d], periods[d])
        gath_u[q, d] = u
        colg_u[p, d] = u

    def pass_a(i, carry):
        k = z_step(i)
        slot = slot_of(0, k)
        arrived(a_recv.at[0, (z + k) & (NZ - 1)], gath.at[slot, pl.ds(0, 2)])
        for d in y_order:
            a_then(k, d).start()
        a_phase(slot)
        return carry

    def pass_b(k):
        slot = slot_of(k, 0)
        arrived(b_recv.at[(y + k) & (NY - 1)], gath.at[slot, 2])
        for d in reversed(z_order):
            b_then(k, d).start()
        b_phase(slot)

    def z_step(i):
        half = (i >> 1) + 1
        return (half + (i & 1) * (NZ - 2 * half)) & (NZ - 1)

    lax.fori_loop(0, min(2, NZ - 1), pass_a, 0)
    for k in y_order[:2]:
        pass_b(k)
    lax.fori_loop(min(2, NZ - 1), min(4, NZ - 1), pass_a, 0)
    for k in y_order[2:]:
        pass_b(k)
    lax.fori_loop(min(4, NZ - 1), NZ - 1, pass_a, 0)

    held[...] = jnp.zeros_like(held)
    rolled[...] = jnp.zeros_like(rolled)
    arrived(group_recv.at[0], colg.at[pl.ds(0, NR - 1)])
    for i in range(1, NR):
        slot = (p + i) & (NR - 1)
        for d in range(3):
            colg_u[slot, d] = to_phase(colg[slot, d], periods[d])

    def a_rest(k):
        for d in y_order:
            a_phase(slot_of(d, k))

    def rest(i, carry):
        k = z_step(i)
        arrived(a_recv.at[1, (z + k) & (NZ - 1)], gath.at[pl.ds(0, 3 * NY - 2), 2])
        for d in range(NY):
            b_phase(slot_of(d, k))
        a_rest(k)
        return carry

    arrived(a_recv.at[1, z], gath.at[pl.ds(0, NY - 1), pl.ds(0, 2)])
    a_rest(0)
    lax.fori_loop(0, NZ - 1, rest, 0)

    def head(t, rowed, skewed):
        r = tl[0, OWN + t]
        c = tl[1, OWN + t]
        for d in range(3):
            row = jnp.broadcast_to(gath_u[r >> 4, d, pl.ds(r & 15, 1), :], (8, BLK))
            rowed[0, d] = row
            for k in range(1, 4):
                rowed[k, d] = pltpu.roll(row, BLK - 8 * k, 1)
            column = colg_u[c >> 4, d, pl.ds(c & 15, 1), :]
            for k, shift in enumerate(FAR_SHIFTS):
                skewed[k, d] = skew(column, shift)

    def r1_copy(b, d):
        return copy(
            prs.at[b, y], prs.at[b, y], sent.at[4], r1_recv.at[b // (BATCHES - 1)], at_y(d)
        )

    def finish(t):
        for d in range(3):
            at = pl.ds(t % GROUP, 1)
            prs[t // GROUP, y, d, at, :] = fold(rolled[d])
            cparts[t // GROUP, d, at, :] = fold(unskew(rolled[3 + d], index))

    def settle():
        for d in range(3):
            rolled[d] = settle_row([held[k, d] for k in range(4)])
            rolled[3 + d] = settle_column([held[4 + k, d] for k in range(4)], FAR_SHIFTS)

    def far_step(t, rowed, skewed, next_rowed, next_skewed):
        head(jnp.minimum(t + 1, FAR - 1), next_rowed, next_skewed)
        finish(jnp.maximum(t - 2, 0))
        settle()
        r = tl[0, OWN + t]
        c = tl[1, OWN + t]
        same = p * (NY * NZ * OWN) + r == ((c >> 4) * (NY * NZ) + q) * OWN + (c & 15)
        extra = jnp.where((sub == 0) & same, 1e6, 0.0)
        rows = [[rowed[k, d] for d in range(3)] for k in range(4)]
        columns = [[skewed[k, d] for d in range(3)] for k in range(4)]
        to_rows, to_columns = meet(rows, columns, scales, extra, None)
        for k in range(4):
            for d in range(3):
                held[k, d] = to_rows[k][d]
                held[4 + k, d] = to_columns[k][d]

    def far_steps(i, carry):
        far_step(2 * i, rowed.at[0], skewed.at[0], rowed.at[1], skewed.at[1])
        far_step(2 * i + 1, rowed.at[1], skewed.at[1], rowed.at[0], skewed.at[0])
        return carry

    def batch(b, carry):
        start = b * (GROUP // 2)
        lax.fori_loop(start, start + GROUP // 2, far_steps, 0)

        @pl.when(b > 0)
        def _():
            for d in y_order:
                r1_copy(b - 1, d).start()

        return carry

    head(0, rowed.at[0], skewed.at[0])
    lax.fori_loop(0, BATCHES, batch, 0)
    finish(FAR - 2)
    settle()
    finish(FAR - 1)
    for d in reversed(y_order):
        r1_copy(BATCHES - 1, d).start()

    r = tlv[0:1, OWN : OWN + FAR]
    c = tlv[1:2, OWN : OWN + FAR]
    same = p * (NY * NZ * OWN) + r == ((c >> 4) * (NY * NZ) + q) * OWN + (c & 15)
    rows = lax.broadcasted_iota(jnp.int32, (NR * OWN, FAR), 0)
    minus = jnp.where((rows == c) & jnp.logical_not(same), -1.0, 0.0).astype(jnp.bfloat16)
    for d in range(3):
        full = spread(minus, cparts[:, d].reshape(FAR, BLK))
        coltot[:, d] = full.reshape(NR, OWN, BLK)

    def rc_copy(d):
        to = (p + d) & (NR - 1)
        return copy(coltot.at[to], crs.at[p], sent.at[5], group_recv.at[2], at_row(d))

    for d in range(1, NR):
        rc_copy(d).start()

    arrived(sent.at[0], gath.at[pl.ds(0, NY * NZ - 1), pl.ds(0, 2)])
    arrived(sent.at[1], gath.at[pl.ds(0, NY * NZ - 1), 2])
    arrived(sent.at[2], colg.at[pl.ds(0, NR - 1)])
    arrived(sent.at[3], meta.at[pl.ds(0, NY - 1)])

    def self_tile(k):
        u = [gath_u[q, d, pl.ds(k, 1), :] for d in range(3)]
        wide = [jnp.broadcast_to(v, (8, BLK)) for v in u]
        rows = [wide, [pltpu.roll(v, BLK - 8, 1) for v in wide]]
        columns = [[skew(v, shift) for v in u] for shift in SELF_SHIFTS]
        to_rows, to_columns = meet(rows, columns, scales, None, sub < 7)
        for d in range(3):
            force = settle_row([v[d] for v in to_rows])
            force -= unskew(settle_column([v[d] for v in to_columns], SELF_SHIFTS), index)
            own_f[d, pl.ds(k, 1), :] = strength * fold(force)

    def self_tiles(i, carry):
        self_tile(2 * i)
        self_tile(2 * i + 1)
        return carry

    lax.fori_loop(0, OWN // 2, self_tiles, 0)

    arrived(group_recv.at[1], meta.at[pl.ds(0, NY - 1)])

    def chosen(lo, hi):
        names = jnp.concatenate(
            [meta[i, 0:1, b * GROUP : (b + 1) * GROUP] for b in range(lo, hi) for i in range(NY)],
            axis=1,
        )
        count = NY * GROUP * (hi - lo)
        mine = lax.broadcasted_iota(jnp.int32, (NZ * OWN, count), 0) + y * (NZ * OWN)
        return jnp.where(mine.astype(jnp.float32) == names, 1.0, 0.0).astype(jnp.bfloat16)

    last = BATCHES - 1
    early = chosen(0, last)
    late = chosen(last, BATCHES)
    arrived(r1_recv.at[0], prs.at[pl.ds(0, last), pl.ds(0, NY - 1)])
    for d in range(3):
        full = spread(early, prs[0:last, :, d].reshape(last * NY * GROUP, BLK))
        totals[:, d] = full.reshape(NZ, OWN, BLK)
    arrived(r1_recv.at[1], prs.at[last, pl.ds(0, NY - 1)])
    for d in range(3):
        full = spread(late, prs[last, :, d].reshape(NY * GROUP, BLK))
        totals[:, d] += full.reshape(NZ, OWN, BLK)

    def r2_copy(d):
        to = (z + d) & (NZ - 1)
        return copy(totals.at[to], rs2.at[z], sent.at[6], group_recv.at[3], at_z(d))

    for d in reversed(z_order):
        r2_copy(d).start()

    x = [gath[q, d] for d in range(3)]
    order = chain[...]
    order_t = jnp.transpose(order.astype(jnp.float32))
    lane_f = lax.broadcasted_iota(jnp.int32, (BLK, BLK), 1).astype(jnp.float32)
    sub_f = lax.broadcasted_iota(jnp.int32, (BLK, BLK), 0).astype(jnp.float32)
    for b in range(OWN):
        hit = order_t[:, b : b + 1] == lane_f
        inv[b : b + 1, :] = jnp.sum(jnp.where(hit, sub_f, 0.0), axis=0, keepdims=True)
    back = inv[...].astype(jnp.int32)
    ordered = [jnp.take_along_axis(v, order, axis=1, mode="promise_in_bounds") for v in x]
    bond = [pltpu.roll(v, BLK - 1, 1) - v for v in ordered]
    squared = bond[0] * bond[0] + bond[1] * bond[1] + bond[2] * bond[2]
    rank = lax.broadcasted_iota(jnp.int32, (OWN, BLK), 1) + 1
    stiffness = -spring / jnp.maximum(1.0 - squared / (bond_reach * bond_reach), 0.3)
    stiffness = jnp.where(rank % CHAIN != 0, stiffness, 0.0)
    for d in range(3):
        pulled = bond[d] * stiffness
        along = pltpu.roll(pulled, 1, 1) - pulled
        own_f[d] += jnp.take_along_axis(along, back, axis=1, mode="promise_in_bounds")

    arrived(sent.at[4], prs.at[:, pl.ds(0, NY - 1)])
    arrived(sent.at[5], crs.at[pl.ds(0, NR - 1)])
    arrived(group_recv.at[2], crs.at[pl.ds(0, NR - 1)])
    acc = [coltot[p, d] + totals[z, d] for d in range(3)]
    for i in range(1, NR):
        slot = (p + i) & (NR - 1)
        acc = [acc[d] + crs[slot, d] for d in range(3)]
    arrived(group_recv.at[3], rs2.at[pl.ds(0, NZ - 1)])
    for i in range(1, NZ):
        slot = (z + i) & (NZ - 1)
        acc = [acc[d] + rs2[slot, d] for d in range(3)]
    for d in range(3):
        total = strength * acc[d] + own_f[d]
        for b in range(OWN):
            out[d : d + 1, b * BLK : (b + 1) * BLK] = total[b : b + 1, :]
    arrived(sent.at[6], totals.at[pl.ds(0, NZ - 1)])


def on_device(NR, NY, NZ, positions, velocities, chain_order, tile_list):
    f32, i32 = jnp.float32, jnp.int32
    dma = pltpu.SemaphoreType.DMA
    in_hbm = pl.BlockSpec(memory_space=pltpu.HBM)
    forces = pl.pallas_call(
        functools.partial(kernel, NR, NY, NZ),
        out_shape=jax.ShapeDtypeStruct(positions.shape, f32),
        in_specs=[in_hbm] * 3,
        out_specs=pl.BlockSpec(memory_space=pltpu.VMEM),
        scratch_shapes=[
            pltpu.SMEM(tile_list.shape, i32),
            pltpu.VMEM(tile_list.shape, i32),
            pltpu.VMEM(positions.shape, f32),
            pltpu.VMEM((OWN, BLK), i32),
            pltpu.VMEM((NY * NZ, 3, OWN, BLK), f32),
            pltpu.VMEM((NR, 3, OWN, BLK), f32),
            pltpu.VMEM((NY * NZ, 3, OWN, BLK), i32),
            pltpu.VMEM((NR, 3, OWN, BLK), i32),
            pltpu.VMEM((2, 4, 3, 8, BLK), i32),
            pltpu.VMEM((2, 4, 3, 8, BLK), i32),
            pltpu.VMEM((8, 3, 8, BLK), f32),
            pltpu.VMEM((6, 8, BLK), f32),
            pltpu.VMEM((3, OWN, BLK), f32),
            pltpu.VMEM((OWN, BLK), f32),
            pltpu.VMEM((NY, 8, BLK), f32),
            pltpu.VMEM((BATCHES, NY, 3, GROUP, BLK), f32),
            pltpu.VMEM((BATCHES, 3, GROUP, BLK), f32),
            pltpu.VMEM((NZ, 3, OWN, BLK), f32),
            pltpu.VMEM((NR, 3, OWN, BLK), f32),
            pltpu.VMEM((NZ, 3, OWN, BLK), f32),
            pltpu.VMEM((NR, 3, OWN, BLK), f32),
            dma((4,)),
            dma((7,)),
            dma((2, NZ)),
            dma((NY,)),
            dma((4,)),
            dma((2,)),
        ],
        compiler_params=pltpu.CompilerParams(
            collective_id=0, has_side_effects=True, vmem_limit_bytes=32 * 1024 * 1024
        ),
    )(*[pltpu.with_memory_space_constraint(v, pltpu.HBM) for v in (tile_list, positions, chain_order)])
    new_velocity = velocities + time_step * forces
    new_position = positions + time_step * new_velocity
    return (new_velocity, new_position)


def solution(mesh, NZ=8):
    in_specs = (
        P(None, ("row", "col")),
        P(None, ("row", "col")),
        P(("row", "col"), None),
        P(None, ("row", "col")),
    )
    out_specs = (P(None, ("row", "col")), P(None, ("row", "col")))
    return jax.shard_map(
        functools.partial(on_device, mesh.shape["row"], mesh.shape["col"] // NZ, NZ),
        mesh=mesh,
        in_specs=in_specs,
        out_specs=out_specs,
        check_vma=False,
    )
```
